128 devices in a mesh: inner: 32 (over z, x, core), outer: 4 (over y).
Axes of the slice: x: 4, y: 4, z: 4, core: 2. Of those that a mesh axis runs over, the one named last changes fastest.
Arguments:
- points: bfloat16 [4, 524288, 64], P('outer', 'inner'), may hold values from -1.5 to 1.5
- charges: bfloat16 [4, 524288, 16], P('outer', 'inner'), may hold values from -6 to 6
- bases: bfloat16 [4, 524288, 128], P('outer', 'inner'), may hold values from -0.25 to 0.25
- transfers: bfloat16 [4, 1024, 128, 128], P('outer', 'inner'), may hold values from -0.5 to 0.5
- parents: bfloat16 [4, 32, 128, 128], P('outer', 'inner'), may hold values from -0.5 to 0.5
- couplings: bfloat16 [4, 192, 128, 128], P('outer', 'inner'), may hold values from -0.0390625 to 0.0390625
- group_couplings: bfloat16 [4, 4, 128, 128], P('outer'), may hold values from -0.009765625 to 0.009765625
- near_pairs: int32 [4, 3072, 2], P('outer', 'inner'), may hold values from 0 to 39, as said below
- pair_count: int32 [4, 32], P('outer', 'inner'), may hold values from 1 to 96, as said below
- far_list: int32 [4, 192], P('outer', 'inner'), may hold values from 0 to 31, as said below
Outputs:
- potentials: float32 [4, 524288, 16], P('outer', 'inner')
The draws below stay inside these ranges and needn't reach their ends.
Inputs may be any that keep to these rules, and one draw needn't show every extreme that they name: `near_pairs`: slot (a, b): a is a holder's leaf; b < 4 names the left inner neighbour's leaf 32 - 4 + b, 4 <= b < 36 the holder's own leaf b - 4 (never a), larger b the right neighbour's leaf b - 36. The first holder of a group names no left neighbour, the last no right one. Slots past the count hold such pairs too and are ignored. `pair_count`: in every group some holder has all 96 slots live. `far_list`: entries are inner indices of nodes in the same group, distinct within a node's list and never the node itself.
All inputs are finite; a program needn't handle non-finite values.
Results may differ from the reference program's by a relative error of at most 0.006.
Values may be sent and summed in bfloat16 or wider, within the bound.
A program may use at most 128 MiB of HBM per device.

```python
import jax
import jax.numpy as jnp
from jax import lax

DIM = 64
LEAF = 512
RANK = 128
NRHS = 16
LEAF_DEV = 32
REACH = 4
FAR = 6
PAIR_BLOCK = 8
SLOTS = 96
LEAVES = 1024
GROUP_POINTS = 524288
N_INNER = 32
N_OUTER = 4


def draw_pair_count(key, part):
    key = jax.random.fold_in(key, 11)
    key_one, key_two = jax.random.split(key)
    uniform_draw = jax.random.randint(key_one, (N_OUTER, N_INNER), 0, SLOTS)
    tally_values = 1 + uniform_draw * uniform_draw // SLOTS
    fullest = jax.random.randint(key_two, (N_OUTER, 1), 0, N_INNER)
    location_index = jnp.arange(N_INNER, dtype=jnp.int32)[None, :]
    return jnp.where(location_index == fullest, SLOTS, tally_values).astype(jnp.int32)


def draw_near_pairs(key, part):
    key = jax.random.fold_in(key, 23)
    key_one, key_two, key_three, key_four = jax.random.split(key, 4)
    lattice_shape = (N_OUTER, N_INNER, SLOTS)
    first_leaf = jax.random.randint(key_one, lattice_shape, 0, LEAF_DEV)
    side_pick = jax.random.randint(key_two, lattice_shape, 0, 3)
    location_index = jnp.arange(N_INNER, dtype=jnp.int32)[None, :, None]
    side_pick = jnp.where((side_pick == 0) & (location_index == 0), 1, side_pick)
    side_pick = jnp.where((side_pick == 2) & (location_index == N_INNER - 1), 1, side_pick)
    stride = jax.random.randint(key_three, lattice_shape, 1, LEAF_DEV)
    own_leaf = REACH + (first_leaf + stride) % LEAF_DEV
    rim_leaf = jax.random.randint(key_four, lattice_shape, 0, REACH)
    second_leaf = jnp.where(side_pick == 0, rim_leaf, jnp.where(side_pick == 2, REACH + LEAF_DEV + rim_leaf, own_leaf))
    stacked = jnp.stack([first_leaf, second_leaf], -1)
    return stacked.reshape(N_OUTER, N_INNER * SLOTS, 2).astype(jnp.int32)


def draw_far_list(key, part):
    key = jax.random.fold_in(key, 37)
    node_keys = jax.random.split(key, N_OUTER * N_INNER)
    offsets = jax.vmap(lambda node_key: jax.random.permutation(node_key, N_INNER - 1)[:FAR])(node_keys)
    node_ids = jnp.arange(N_OUTER * N_INNER, dtype=jnp.int32) % N_INNER
    entries = (node_ids[:, None] + 1 + offsets) % N_INNER
    return entries.reshape(N_OUTER, N_INNER * FAR).astype(jnp.int32)


def steps_of(rng, dims, cuts, smallest, high):
    gain = 1.0
    for axis_at, shards_of in cuts:
        draws = jax.random.uniform(jax.random.fold_in(jax.random.fold_in(rng, 6), axis_at), (shards_of,), jnp.float32, smallest / len(cuts), high / len(cuts))
        gain = gain * jnp.repeat(jnp.exp(draws), dims[axis_at] // shards_of).reshape((-1,) + (1,) * (len(dims) - 1 - axis_at))
    return gain


def gaussian(key, shape, deviation, most, shards=(), kind=jnp.bfloat16):
    values = jax.random.normal(key, shape, jnp.float32) * deviation
    if len(shards) > 0:
        values = steps_of(key, shape, shards, -0.22, 0.18) * values
    return jnp.clip(values, min=-most, max=most).astype(kind)


def setup_inputs(seed: int = 0) -> dict:
    key_list = jax.random.split(jax.random.key(seed), 11)
    points = gaussian(key_list[0], (N_OUTER, GROUP_POINTS, DIM), 0.25, 1.5, ((0, 4), (1, 32)))
    charges = gaussian(key_list[1], (N_OUTER, GROUP_POINTS, NRHS), 1.0, 6.0, ((0, 4), (1, 32)))
    bases = gaussian(key_list[2], (N_OUTER, GROUP_POINTS, RANK), LEAF ** -0.5, 0.25, ((0, 4), (1, 32)))
    transfers = gaussian(key_list[3], (N_OUTER, LEAVES, RANK, RANK), RANK ** -0.5, 0.5, ((0, 4), (1, 32)))
    parents = gaussian(key_list[4], (N_OUTER, N_INNER, RANK, RANK), RANK ** -0.5, 0.5, ((0, 4), (1, 32)))
    couplings = gaussian(key_list[5], (N_OUTER, N_INNER * FAR, RANK, RANK), (RANK * FAR * LEAF_DEV) ** -0.5, 0.0390625, ((0, 4), (1, 32)))
    group_couplings = gaussian(key_list[6], (N_OUTER, N_OUTER, RANK, RANK), (RANK * (N_OUTER - 1) * LEAF_DEV * N_INNER) ** -0.5, 0.009765625, ((0, 4),))
    near_pairs = draw_near_pairs(jax.random.fold_in(key_list[10], 71), 0)
    pair_count = draw_pair_count(jax.random.fold_in(key_list[10], 71), 0)
    far_list = draw_far_list(jax.random.fold_in(key_list[10], 71), 0)
    return dict(points=points, charges=charges, bases=bases, transfers=transfers, parents=parents, couplings=couplings, group_couplings=group_couplings, near_pairs=near_pairs, pair_count=pair_count, far_list=far_list)


INV_TWO_BAND = 0.5
RIDGE = 0.25


def kernel_tiles(left_samples, right_samples):
    left_expanded = left_samples.astype(jnp.float32)
    right_expanded = right_samples.astype(jnp.float32)
    left_square = jnp.sum(left_expanded * left_expanded, -1)
    right_square = jnp.sum(right_expanded * right_expanded, -1)
    cross_kernel = jnp.einsum('nom,nwm->now', left_expanded, right_expanded)
    distance = left_square[:, :, None] + right_square[:, None, :] - 2.0 * cross_kernel
    return jnp.exp(-INV_TWO_BAND * distance).astype(jnp.bfloat16)


def widen(blocks):
    blank = jnp.zeros((N_OUTER, 1, REACH) + blocks.shape[3:], blocks.dtype)
    from_prev = jnp.concatenate([blank, blocks[:, :-1, LEAF_DEV - REACH:]], 1)
    from_next = jnp.concatenate([blocks[:, 1:, :REACH], blank], 1)
    return jnp.concatenate([from_prev, blocks, from_next], 2)


def device_near(operands):
    wide_points, wide_charges, pair_list, live_count = operands
    pair_blocks = pair_list.reshape(SLOTS // PAIR_BLOCK, PAIR_BLOCK, 2)

    def one_block(totals, block_index):
        chosen = pair_blocks[block_index]
        first_slot = chosen[:, 0] + REACH
        second_slot = chosen[:, 1]
        slot_ids = block_index * PAIR_BLOCK + jnp.arange(PAIR_BLOCK, dtype=jnp.int32)
        live_mask = (slot_ids < live_count).astype(jnp.float32)
        kernel = kernel_tiles(wide_points[first_slot], wide_points[second_slot]).astype(jnp.float32)
        to_first = jnp.einsum('bpq,bqn->bpn', kernel, wide_charges[second_slot].astype(jnp.float32))
        to_second = jnp.einsum('bpq,bpn->bqn', kernel, wide_charges[first_slot].astype(jnp.float32))
        totals = totals.at[first_slot].add(to_first * live_mask[:, None, None])
        totals = totals.at[second_slot].add(to_second * live_mask[:, None, None])
        return totals, block_index

    start = jnp.zeros((LEAF_DEV + 2 * REACH, LEAF, NRHS), jnp.float32)
    return lax.scan(one_block, start, jnp.arange(SLOTS // PAIR_BLOCK, dtype=jnp.int32))[0]


def diag_block(operands):
    block_points, block_charges = operands
    kernel = kernel_tiles(block_points, block_points).astype(jnp.float32)
    return jnp.einsum('bpq,bqn->bpn', kernel, block_charges.astype(jnp.float32))


def reference(points, charges, bases, transfers, parents, couplings, group_couplings, near_pairs, pair_count, far_list):
    devices = N_OUTER * N_INNER
    point_grid = points.reshape(N_OUTER, N_INNER, LEAF_DEV, LEAF, DIM)
    charge_grid = charges.reshape(N_OUTER, N_INNER, LEAF_DEV, LEAF, NRHS)
    wide_points = widen(point_grid).reshape(devices, LEAF_DEV + 2 * REACH, LEAF, DIM)
    wide_charges = widen(charge_grid).reshape(devices, LEAF_DEV + 2 * REACH, LEAF, NRHS)
    totals = lax.map(device_near, (wide_points, wide_charges, near_pairs.reshape(devices, SLOTS, 2), pair_count.reshape(devices)))
    totals = totals.reshape(N_OUTER, N_INNER, LEAF_DEV + 2 * REACH, LEAF, NRHS)
    own_part = totals[:, :, REACH:REACH + LEAF_DEV]
    blank = jnp.zeros((N_OUTER, 1, REACH, LEAF, NRHS), jnp.float32)
    from_left = jnp.concatenate([blank, totals[:, :-1, REACH + LEAF_DEV:]], 1)
    from_right = jnp.concatenate([totals[:, 1:, :REACH], blank], 1)
    own_part = own_part.at[:, :, :REACH].add(from_left)
    own_part = own_part.at[:, :, LEAF_DEV - REACH:].add(from_right)
    diagonal = lax.map(diag_block, (points.reshape(-1, PAIR_BLOCK, LEAF, DIM), charges.reshape(-1, PAIR_BLOCK, LEAF, NRHS)))
    near_field = own_part.reshape(N_OUTER, N_INNER, LEAF_DEV, LEAF, NRHS) + diagonal.reshape(N_OUTER, N_INNER, LEAF_DEV, LEAF, NRHS)

    leaf_bases = bases.reshape(N_OUTER, N_INNER, LEAF_DEV, LEAF, RANK).astype(jnp.float32)
    leaf_transfers = transfers.reshape(N_OUTER, N_INNER, LEAF_DEV, RANK, RANK).astype(jnp.float32)
    parent_maps = parents.astype(jnp.float32)
    leaf_skeleton = jnp.einsum('gilpr,gilpn->gilrn', leaf_bases, charge_grid.astype(jnp.float32)).astype(jnp.bfloat16)
    node_skeleton = jnp.einsum('gilrs,gilrn->gisn', leaf_transfers, leaf_skeleton.astype(jnp.float32)).astype(jnp.bfloat16)
    group_skeleton = jnp.einsum('girs,girn->gsn', parent_maps, node_skeleton.astype(jnp.float32)).astype(jnp.bfloat16)
    others = 1.0 - jnp.eye(N_OUTER, dtype=jnp.float32)
    group_field = jnp.einsum('ghrs,hsn->grn', group_couplings.astype(jnp.float32) * others[:, :, None, None], group_skeleton.astype(jnp.float32)).astype(jnp.bfloat16)
    lists = far_list.reshape(N_OUTER, N_INNER, FAR)
    chosen = jax.vmap(lambda nodes, entries: nodes[entries])(node_skeleton, lists)
    coupling_grid = couplings.reshape(N_OUTER, N_INNER, FAR, RANK, RANK).astype(jnp.float32)
    node_field = jnp.einsum('gijrs,gijsn->girn', coupling_grid, chosen.astype(jnp.float32))
    node_field = (node_field + jnp.einsum('girs,gsn->girn', parent_maps, group_field.astype(jnp.float32))).astype(jnp.bfloat16)
    leaf_field = jnp.einsum('gilrs,gisn->gilrn', leaf_transfers, node_field.astype(jnp.float32)).astype(jnp.bfloat16)
    far_field = jnp.einsum('gilpr,gilrn->gilpn', leaf_bases, leaf_field.astype(jnp.float32))
    result = RIDGE * charge_grid.astype(jnp.float32) + near_field + far_field
    return result.reshape(N_OUTER, N_INNER * LEAF_DEV * LEAF, NRHS)
```

```python
import functools

import jax
import jax.numpy as jnp
from jax import lax
from jax.experimental import pallas as pl
from jax.experimental.pallas import tpu as pltpu
from jax.sharding import PartitionSpec as P

REACH = 4
RIDGE = 0.25
BF = jnp.bfloat16
F32 = jnp.float32
DEPTH = 128
VMEM = pl.BlockSpec(memory_space=pltpu.VMEM)
SMEM = pl.BlockSpec(memory_space=pltpu.SMEM)
PARAMS = pltpu.CompilerParams(vmem_limit_bytes=56 * 2**20)


def dot(left, right, left_dim, right_dim):
    return lax.dot_general(
        left, right, (((left_dim,), (right_dim,)), ((), ())), preferred_element_type=F32
    )


def half_square(block):
    wide = block.astype(F32)
    total = 0.5 * jnp.sum(wide * wide, 0, keepdims=True)
    high = total.astype(BF).astype(F32)
    rest = total - high
    middle = rest.astype(BF).astype(F32)
    low = rest - middle
    return high, middle, low


def augment(block, first):
    dim, count = block.shape
    parts = half_square(block)
    row = lax.broadcasted_iota(jnp.int32, (DEPTH - dim, count), 0)
    at = 0 if first else 3
    extra = jnp.where((row >= 3 - at) & (row < 6 - at), 1.0, 0.0)
    for k in range(3):
        extra = jnp.where(row == at + k, -parts[k], extra)
    return jnp.concatenate([block, extra.astype(BF)], 0)


def skeleton_kernel(bases, charges, transfers, parent, node, term):
    leaves, leaf, _ = bases.shape

    def step(index, total):
        cols = pl.ds(pl.multiple_of(index * leaf, leaf), leaf)
        skeleton = dot(charges[:, cols], bases[index], 1, 0).astype(BF)
        return total + dot(skeleton, transfers[index], 1, 0)

    total = lax.fori_loop(
        0, leaves, step, jnp.zeros((charges.shape[0], transfers.shape[2]), F32), unroll=4
    )
    node[...] = total.astype(BF)
    term[...] = dot(total.astype(BF), parent[...], 1, 0)


def split_pairs(pairs, count, halo_list, own_list, leaves):
    def step(index, counts):
        halo_count, own_count = counts
        first, second = pairs[0, index], pairs[1, index]
        own = ((second >= REACH) & (second < REACH + leaves)).astype(jnp.int32)
        code = first * 64 + second
        halo_list[halo_count] = code
        own_list[own_count] = code
        return halo_count + 1 - own, own_count + own

    return lax.fori_loop(0, count, step, (jnp.int32(0), jnp.int32(0)))


def grouped(count, body, group):
    def block(index, carry):
        for k in range(group):
            body(index * group + k)
        return carry

    whole = count // group
    lax.fori_loop(0, whole, block, 0)

    def single(index, carry):
        body(index)
        return carry

    lax.fori_loop(whole * group, count, single, 0)


def halo_kernel(
    pairs, live, points, charges, halo_points, halo_charges,
    first_out, totals, halo_totals,
    second, halo_list, own_list,
):
    leaves, leaf, _ = first_out.shape
    totals[...] = jnp.zeros_like(totals)
    halo_totals[...] = jnp.zeros_like(halo_totals)

    def build(index, carry):
        cols = pl.ds(pl.multiple_of(index * leaf, leaf), leaf)
        first_out[index] = augment(points[:, cols], True).T
        return carry

    lax.fori_loop(0, leaves, build, 0)

    def build_halo(index, carry):
        cols = pl.ds(pl.multiple_of(index * leaf, leaf), leaf)
        second[index] = augment(halo_points[:, cols], False)
        return carry

    lax.fori_loop(0, 2 * REACH, build_halo, 0)
    halo_count, _ = split_pairs(pairs, live[0, 0], halo_list, own_list, leaves)

    def body(index):
        code = halo_list[index]
        a, b = code // 64, code % 64
        b = jnp.where(b < REACH, b, b - leaves)
        cols_a = pl.ds(pl.multiple_of(a * leaf, leaf), leaf)
        cols_b = pl.ds(pl.multiple_of(b * leaf, leaf), leaf)
        tile = jnp.exp(dot(first_out[a], second[b], 1, 0)).astype(BF)
        halo_totals[:, cols_b] += dot(charges[:, cols_a], tile, 1, 0)
        totals[:, cols_a] += dot(halo_charges[:, cols_b], tile, 1, 1)

    grouped(halo_count, body, 4)


def own_kernel(
    pairs, live, points, charges, first, start,
    totals,
    second, halo_list, own_list,
):
    leaves, leaf, _ = first.shape

    def build(index, carry):
        cols = pl.ds(pl.multiple_of(index * leaf, leaf), leaf)
        second[index] = augment(points[:, cols], False)
        return carry

    lax.fori_loop(0, leaves, build, 0)

    def diagonal(index, carry):
        cols = pl.ds(pl.multiple_of(index * leaf, leaf), leaf)
        tile = jnp.exp(dot(first[index], second[index], 1, 0)).astype(BF)
        own = charges[:, cols]
        totals[:, cols] = start[:, cols] + RIDGE * own.astype(F32) + dot(own, tile, 1, 0)
        return carry

    lax.fori_loop(0, leaves, diagonal, 0, unroll=4)
    _, own_count = split_pairs(pairs, live[0, 0], halo_list, own_list, leaves)

    def body(index):
        code = own_list[index]
        a, b = code // 64, code % 64 - REACH
        cols_a = pl.ds(pl.multiple_of(a * leaf, leaf), leaf)
        cols_b = pl.ds(pl.multiple_of(b * leaf, leaf), leaf)
        tile = jnp.exp(dot(first[a], second[b], 1, 0)).astype(BF)
        totals[:, cols_b] += dot(charges[:, cols_a], tile, 1, 0)
        totals[:, cols_a] += dot(charges[:, cols_b], tile, 1, 1)

    grouped(own_count, body, 4)


def finish_kernel(
    bases, transfers, parent, couplings, group_couplings, nodes, groups, far, weight, near, low, high,
    out,
):
    leaves, leaf, _ = bases.shape
    group_field = sum(
        dot(groups[h], group_couplings[h] * weight[h].astype(BF), 1, 1)
        for h in range(groups.shape[0])
    ).astype(BF)
    field = dot(group_field, parent[...], 1, 1)
    for j in range(couplings.shape[0]):
        field += dot(nodes[far[0, j]], couplings[j], 1, 1)
    field = field.astype(BF)
    rim = REACH * leaf

    def step(index, carry):
        cols = pl.ds(pl.multiple_of(index * leaf, leaf), leaf)
        leaf_field = dot(field, transfers[index], 1, 1).astype(BF)
        out[:, cols] = near[:, cols] + dot(leaf_field, bases[index], 1, 1)
        return carry

    lax.fori_loop(0, leaves, step, 0, unroll=4)
    out[:, :rim] += low[...]
    out[:, out.shape[1] - rim :] += high[...]


def on_device(
    points, charges, bases, transfers, parents, couplings, group_couplings, near_pairs, pair_count, far_list
):
    leaves = transfers.shape[1]
    count = points.shape[1]
    leaf = count // leaves
    dim, rhs, rank = points.shape[2], charges.shape[2], bases.shape[2]
    slots = near_pairs.shape[1]
    rim = REACH * leaf
    pt = jnp.swapaxes(points[0], 0, 1)
    ct = jnp.swapaxes(charges[0], 0, 1)
    pairs = jnp.swapaxes(near_pairs[0], 0, 1)
    size = lax.axis_size("inner")
    forward = [(i, i + 1) for i in range(size - 1)]
    backward = [(i + 1, i) for i in range(size - 1)]

    joined = jnp.concatenate([pt, ct], 0)
    low = lax.ppermute(joined[:, count - rim :], "inner", forward)
    high = lax.ppermute(joined[:, :rim], "inner", backward)

    leaf_bases = bases[0].reshape(leaves, leaf, rank)
    node, term = pl.pallas_call(
        skeleton_kernel,
        out_shape=[
            jax.ShapeDtypeStruct((rhs, rank), BF),
            jax.ShapeDtypeStruct((rhs, rank), F32),
        ],
        in_specs=[VMEM] * 4,
        out_specs=[VMEM] * 2,
        compiler_params=PARAMS,
        cost_estimate=pl.CostEstimate(flops=10**9, bytes_accessed=6 * 2**20, transcendentals=0),
        name="skeleton",
    )(leaf_bases, ct, transfers[0], parents[0, 0])
    all_nodes = lax.all_gather(node[None], "inner", axis=0, tiled=True)
    group_total = lax.psum(term, "inner").astype(BF)
    groups = lax.all_gather(group_total[None], "outer", axis=0, tiled=True)

    halo = jnp.concatenate([low, high], 1)
    lists = [pltpu.SMEM((slots + 1,), jnp.int32)] * 2
    first, totals, halo_totals = pl.pallas_call(
        halo_kernel,
        out_shape=[
            jax.ShapeDtypeStruct((leaves, leaf, DEPTH), BF),
            jax.ShapeDtypeStruct((rhs, count), F32),
            jax.ShapeDtypeStruct((rhs, 2 * rim), F32),
        ],
        in_specs=[SMEM, SMEM] + [VMEM] * 4,
        out_specs=[VMEM] * 3,
        scratch_shapes=[pltpu.VMEM((2 * REACH, DEPTH, leaf), BF)] + lists,
        compiler_params=PARAMS,
        cost_estimate=pl.CostEstimate(
            flops=64 * 10**9, bytes_accessed=8 * 2**20, transcendentals=64 * leaf * leaf
        ),
        name="halo_pairs",
    )(pairs, pair_count, pt, ct, halo[:dim], halo[dim:])
    back_low = lax.ppermute(halo_totals[:, rim:], "inner", forward)
    back_high = lax.ppermute(halo_totals[:, :rim], "inner", backward)
    near = pl.pallas_call(
        own_kernel,
        out_shape=jax.ShapeDtypeStruct((rhs, count), F32),
        in_specs=[SMEM, SMEM] + [VMEM] * 4,
        out_specs=VMEM,
        scratch_shapes=[pltpu.VMEM((leaves, DEPTH, leaf), BF)] + lists,
        compiler_params=PARAMS,
        cost_estimate=pl.CostEstimate(
            flops=64 * 10**9, bytes_accessed=8 * 2**20, transcendentals=64 * leaf * leaf
        ),
        name="own_pairs",
    )(pairs, pair_count, pt, ct, first, totals)
    own_group = lax.axis_index("outer")
    weight = (jnp.arange(lax.axis_size("outer"), dtype=jnp.int32) != own_group).astype(F32)
    out = pl.pallas_call(
        finish_kernel,
        out_shape=jax.ShapeDtypeStruct((rhs, count), F32),
        in_specs=[VMEM] * 7 + [SMEM, SMEM] + [VMEM] * 3,
        out_specs=VMEM,
        compiler_params=PARAMS,
        cost_estimate=pl.CostEstimate(flops=10**9, bytes_accessed=8 * 2**20, transcendentals=0),
        name="finish",
    )(
        leaf_bases, transfers[0], parents[0, 0], couplings[0], group_couplings[0],
        all_nodes, groups, far_list, weight, near, back_low, back_high,
    )
    return jnp.swapaxes(out, 0, 1)[None]


def solution(mesh):
    placed = (
        P("outer", "inner", None),
        P("outer", "inner", None),
        P("outer", "inner", None),
        P("outer", "inner", None, None),
        P("outer", "inner", None, None),
        P("outer", "inner", None, None),
        P("outer", None, None, None),
        P("outer", "inner", None),
        P("outer", "inner"),
        P("outer", "inner"),
    )
    return jax.shard_map(
        on_device, mesh=mesh, in_specs=placed, out_specs=P("outer", "inner", None), check_vma=False
    )
```

```python
import functools

import jax
import jax.numpy as jnp
from jax import lax
from jax.experimental import pallas as pl
from jax.experimental.pallas import tpu as pltpu
from jax.sharding import PartitionSpec as P

REACH = 4
RIDGE = 0.25
EXTRA = 16
GROUP = 4
BF = jnp.bfloat16
F32 = jnp.float32
VMEM = pl.BlockSpec(memory_space=pltpu.VMEM)
SMEM = pl.BlockSpec(memory_space=pltpu.SMEM)
ANY = pl.BlockSpec(memory_space=pl.ANY)
MESH = pl.DeviceIdType.MESH
LIMIT = 56 * 2**20


def dot(left, right, left_dim, right_dim):
    return lax.dot_general(
        left, right, (((left_dim,), (right_dim,)), ((), ())), preferred_element_type=F32
    )


def norm_rows(block):
    wide = block.astype(F32)
    total = 0.5 * jnp.sum(wide * wide, 0, keepdims=True)
    high = total.astype(BF).astype(F32)
    rest = total - high
    middle = rest.astype(BF).astype(F32)
    parts = (high, middle, rest - middle)
    row = lax.broadcasted_iota(jnp.int32, (EXTRA, block.shape[1]), 0)
    first = jnp.where((row >= 3) & (row < 6), 1.0, 0.0)
    second = jnp.where(row < 3, 1.0, 0.0)
    for k in range(3):
        first = jnp.where(row == k, -parts[k], first)
        second = jnp.where(row == 3 + k, -parts[k], second)
    return first.astype(BF), second.astype(BF)


def columns(index, width):
    return pl.ds(pl.multiple_of(index * width, width), width)


def tile_of(points, firsts, seconds, cols_a, cols_b):
    left = jnp.concatenate([points[:, cols_a], firsts[:, cols_a]], 0)
    right = jnp.concatenate([points[:, cols_b], seconds[:, cols_b]], 0)
    return jnp.exp(dot(left, right, 0, 0)).astype(BF)


def exchange_kernel(
    inner, outer, leaves,
    pt_hbm, ct_hbm, bases_hbm, transfers_hbm, parent, couplings, group_couplings, far,
    halo_points, halo_charges, near, field_out,
    points, charges, bases, transfers, skeletons, packed, slots, group_slots,
    load_sem, halo_send, halo_recv, node_send, node_recv, group_send, group_recv,
):
    me, group = lax.axis_index("inner"), lax.axis_index("outer")
    right, left = lax.rem(me + 1, inner), lax.rem(me + inner - 1, inner)
    rhs, count = ct_hbm.shape
    leaf = count // leaves
    rim = REACH * leaf
    rank = parent.shape[1]
    chunk = 8
    loads = [
        pltpu.make_async_copy(ct_hbm, charges, load_sem.at[0]),
        pltpu.make_async_copy(transfers_hbm, transfers, load_sem.at[1]),
        pltpu.make_async_copy(pt_hbm, points, load_sem.at[2]),
    ]
    base_loads = [
        pltpu.make_async_copy(
            bases_hbm.at[pl.ds(k * chunk, chunk)], bases.at[pl.ds(k * chunk, chunk)], load_sem.at[3 + k]
        )
        for k in range(leaves // chunk)
    ]
    loads[0].start()
    for copy in base_loads:
        copy.start()
    loads[1].start()
    loads[2].start()
    barrier = pltpu.get_barrier_semaphore()
    for k in range(1, inner):
        pl.semaphore_signal(
            barrier, inc=1, device_id={"inner": lax.rem(me + k, inner)}, device_id_type=MESH
        )
    for k in range(1, outer):
        pl.semaphore_signal(
            barrier, inc=1, device_id={"outer": lax.rem(group + k, outer)}, device_id_type=MESH
        )

    loads[0].wait()
    for k, copy in enumerate(base_loads):
        copy.wait()
        for index in range(k * chunk, (k + 1) * chunk):
            block = charges[:, index * leaf : (index + 1) * leaf]
            skeletons[:, index * rank : (index + 1) * rank] = dot(block, bases[index], 1, 0).astype(BF)
    loads[1].wait()
    node = dot(skeletons[...], transfers[...], 1, 0).astype(BF)
    packed[:rhs] = node.astype(F32)
    packed[rhs:] = dot(node, parent[...], 1, 0)
    slots[me] = packed[...]

    pl.semaphore_wait(barrier, inner + outer - 2)

    def node_copy(k):
        return pltpu.make_async_remote_copy(
            src_ref=packed, dst_ref=slots.at[me], send_sem=node_send.at[k], recv_sem=node_recv.at[me],
            device_id={"inner": lax.rem(me + k, inner)}, device_id_type=MESH,
        )

    for k in range(1, inner):
        node_copy(k).start()
    halo_copies = []
    for k, (source, target, peer, begin) in enumerate((
        (pt_hbm, halo_points.at[0], right, count - rim),
        (ct_hbm, halo_charges.at[0], right, count - rim),
        (pt_hbm, halo_points.at[1], left, 0),
        (ct_hbm, halo_charges.at[1], left, 0),
    )):
        copy = pltpu.make_async_remote_copy(
            src_ref=source.at[:, pl.ds(begin, rim)], dst_ref=target,
            send_sem=halo_send.at[k], recv_sem=halo_recv.at[k],
            device_id={"inner": peer}, device_id_type=MESH,
        )
        copy.start()
        halo_copies.append(copy)
    loads[2].wait()

    def diagonal(index, carry):
        cols = columns(index, leaf)
        first, second = norm_rows(points[:, cols])
        left_form = jnp.concatenate([points[:, cols], first], 0)
        right_form = jnp.concatenate([points[:, cols], second], 0)
        tile = jnp.exp(dot(left_form, right_form, 0, 0)).astype(BF)
        own = charges[:, cols]
        near[:, cols] = RIDGE * own.astype(F32) + dot(own, tile, 1, 0)
        return carry

    half = leaves // 2
    lax.fori_loop(0, half, diagonal, 0, unroll=4)

    for k in range(1, inner):
        sender = lax.rem(me + k, inner)
        pltpu.make_async_copy(packed, slots.at[sender], node_recv.at[sender]).wait()
    group_slots[group] = jnp.sum(slots[:, rhs:], 0).astype(BF)

    def group_copy(k):
        return pltpu.make_async_remote_copy(
            src_ref=group_slots.at[group], dst_ref=group_slots.at[group],
            send_sem=group_send.at[k], recv_sem=group_recv.at[group],
            device_id={"outer": lax.rem(group + k, outer)}, device_id_type=MESH,
        )

    for k in range(1, outer):
        group_copy(k).start()
    field = jnp.zeros((rhs, rank), F32)
    for j in range(couplings.shape[0]):
        field += dot(slots[far[0, j], :rhs].astype(BF), couplings[j], 1, 1)
    lax.fori_loop(half, leaves, diagonal, 0, unroll=4)
    group_field = jnp.zeros((rhs, rank), F32)
    for k in range(1, outer):
        sender = lax.rem(group + k, outer)
        pltpu.make_async_copy(group_slots.at[group], group_slots.at[sender], group_recv.at[sender]).wait()
        group_field += dot(group_slots[sender], group_couplings[sender], 1, 1)
    field += dot(group_field.astype(BF), parent[...], 1, 1)
    field_out[...] = field.astype(BF)
    for k in range(1, inner):
        node_copy(k).wait_send()
    for k in range(1, outer):
        group_copy(k).wait_send()
    for copy in halo_copies:
        copy.wait()


def pair_kernel(
    leaves, leaf,
    pairs, live, pt_hbm, ct_hbm, halo_points, halo_charges, near_hbm,
    out_near, out_halo,
    points, charges, firsts, seconds, totals, sem,
):
    rim = REACH * leaf
    count = leaves * leaf
    spots = (pl.ds(0, rim), pl.ds(rim + count, rim))
    own = pl.ds(rim, count)
    copies = [
        pltpu.make_async_copy(pt_hbm, points.at[:, own], sem.at[0]),
        pltpu.make_async_copy(halo_points.at[0], points.at[:, spots[0]], sem.at[1]),
        pltpu.make_async_copy(halo_points.at[1], points.at[:, spots[1]], sem.at[2]),
        pltpu.make_async_copy(ct_hbm, charges.at[:, own], sem.at[3]),
        pltpu.make_async_copy(halo_charges.at[0], charges.at[:, spots[0]], sem.at[4]),
        pltpu.make_async_copy(halo_charges.at[1], charges.at[:, spots[1]], sem.at[5]),
        pltpu.make_async_copy(near_hbm, totals.at[:, own], sem.at[6]),
    ]
    for copy in copies:
        copy.start()
    for spot in spots:
        totals[:, spot] = jnp.zeros((totals.shape[0], rim), F32)
    for copy in copies:
        copy.wait()

    def build(index, carry):
        cols = columns(index, leaf)
        firsts[:, cols], seconds[:, cols] = norm_rows(points[:, cols])
        return carry

    lax.fori_loop(0, leaves + 2 * REACH, build, 0, unroll=2)

    def body(index):
        cols_a = columns(pairs[0, index] + REACH, leaf)
        cols_b = columns(pairs[1, index], leaf)
        tile = tile_of(points, firsts, seconds, cols_a, cols_b)
        totals[:, cols_b] += dot(charges[:, cols_a], tile, 1, 0)
        totals[:, cols_a] += dot(charges[:, cols_b], tile, 1, 1)

    def block(index, carry):
        for k in range(GROUP):
            body(index * GROUP + k)
        return carry

    def single(index, carry):
        body(index)
        return carry

    number = live[0, 0]
    whole = number // GROUP
    lax.fori_loop(0, whole, block, 0)
    lax.fori_loop(whole * GROUP, number, single, 0)
    writes = [
        pltpu.make_async_copy(totals.at[:, own], out_near, sem.at[0]),
        pltpu.make_async_copy(totals.at[:, spots[0]], out_halo.at[0], sem.at[1]),
        pltpu.make_async_copy(totals.at[:, spots[1]], out_halo.at[1], sem.at[2]),
    ]
    for copy in writes:
        copy.start()
    for copy in writes:
        copy.wait()


def finish_kernel(
    inner,
    halo, near_hbm, bases_hbm, transfers_hbm, field,
    out,
    near, bases, transfers, leaf_fields, arrived, load_sem, send_sem, recv_sem,
):
    me = lax.axis_index("inner")
    right, left = lax.rem(me + 1, inner), lax.rem(me + inner - 1, inner)
    leaves, leaf, rank = bases.shape
    count = near.shape[1]
    rim = REACH * leaf
    chunk = 8
    barrier = pltpu.get_barrier_semaphore()
    for peer in (left, right):
        pl.semaphore_signal(barrier, inc=1, device_id={"inner": peer}, device_id_type=MESH)
    loads = [
        pltpu.make_async_copy(transfers_hbm, transfers, load_sem.at[0]),
        pltpu.make_async_copy(near_hbm, near, load_sem.at[1]),
    ]
    base_loads = [
        pltpu.make_async_copy(
            bases_hbm.at[pl.ds(k * chunk, chunk)], bases.at[pl.ds(k * chunk, chunk)], load_sem.at[2 + k]
        )
        for k in range(leaves // chunk)
    ]
    for copy in loads + base_loads:
        copy.start()
    loads[0].wait()
    leaf_fields[...] = dot(field[...], transfers[...], 1, 1).astype(BF)
    pl.semaphore_wait(barrier, 2)
    copies = []
    for k, peer in enumerate((left, right)):
        copy = pltpu.make_async_remote_copy(
            src_ref=halo.at[k], dst_ref=arrived.at[1 - k], send_sem=send_sem.at[k],
            recv_sem=recv_sem.at[1 - k], device_id={"inner": peer}, device_id_type=MESH,
        )
        copy.start()
        copies.append(copy)
    loads[1].wait()
    for k, copy in enumerate(base_loads):
        copy.wait()
        for index in range(k * chunk, (k + 1) * chunk):
            span = slice(index * leaf, (index + 1) * leaf)
            part = leaf_fields[:, index * rank : (index + 1) * rank]
            out[:, span] = near[:, span] + dot(part, bases[index], 1, 1)
    for copy in copies:
        copy.wait()
    out[:, :rim] += arrived[0]
    out[:, count - rim :] += arrived[1]


def on_device(
    points, charges, bases, transfers, parents, couplings, group_couplings, near_pairs, pair_count, far_list
):
    leaves = transfers.shape[1]
    count = points.shape[1]
    leaf = count // leaves
    dim, rhs, rank = points.shape[2], charges.shape[2], bases.shape[2]
    rim = REACH * leaf
    wide = count + 2 * rim
    inner, outer = lax.axis_size("inner"), lax.axis_size("outer")
    pt = jnp.swapaxes(points[0], 0, 1)
    ct = jnp.swapaxes(charges[0], 0, 1)
    pairs = jnp.swapaxes(near_pairs[0], 0, 1)
    leaf_bases = bases[0].reshape(leaves, leaf, rank)
    flat_transfers = transfers[0].reshape(leaves * rank, rank)
    dma = pltpu.SemaphoreType.DMA
    halo_points, halo_charges, near, field = pl.pallas_call(
        functools.partial(exchange_kernel, inner, outer, leaves),
        out_shape=[
            jax.ShapeDtypeStruct((2, dim, rim), BF),
            jax.ShapeDtypeStruct((2, rhs, rim), BF),
            jax.ShapeDtypeStruct((rhs, count), F32),
            jax.ShapeDtypeStruct((rhs, rank), BF),
        ],
        in_specs=[ANY] * 4 + [VMEM] * 3 + [SMEM],
        out_specs=[ANY, ANY, VMEM, VMEM],
        scratch_shapes=[
            pltpu.VMEM((dim, count), BF),
            pltpu.VMEM((rhs, count), BF),
            pltpu.VMEM((leaves, leaf, rank), BF),
            pltpu.VMEM((leaves * rank, rank), BF),
            pltpu.VMEM((rhs, leaves * rank), BF),
            pltpu.VMEM((2 * rhs, rank), F32),
            pltpu.VMEM((inner, 2 * rhs, rank), F32),
            pltpu.VMEM((outer, rhs, rank), BF),
            dma((3 + leaves // 8,)),
            dma((4,)),
            dma((4,)),
            dma((inner,)),
            dma((inner,)),
            dma((outer,)),
            dma((outer,)),
        ],
        compiler_params=pltpu.CompilerParams(
            vmem_limit_bytes=LIMIT, collective_id=0, has_side_effects=True
        ),
        name="exchange",
    )(pt, ct, leaf_bases, flat_transfers, parents[0, 0], couplings[0], group_couplings[0], far_list)
    near, halo = pl.pallas_call(
        functools.partial(pair_kernel, leaves, leaf),
        out_shape=[
            jax.ShapeDtypeStruct((rhs, count), F32),
            jax.ShapeDtypeStruct((2, rhs, rim), F32),
        ],
        in_specs=[SMEM, SMEM] + [ANY] * 5,
        out_specs=[ANY] * 2,
        scratch_shapes=[
            pltpu.VMEM((dim, wide), BF),
            pltpu.VMEM((rhs, wide), BF),
            pltpu.VMEM((EXTRA, wide), BF),
            pltpu.VMEM((EXTRA, wide), BF),
            pltpu.VMEM((rhs, wide), F32),
            dma((7,)),
        ],
        compiler_params=pltpu.CompilerParams(vmem_limit_bytes=LIMIT),
        name="pairs",
    )(pairs, pair_count, pt, ct, halo_points, halo_charges, near)
    out = pl.pallas_call(
        functools.partial(finish_kernel, inner),
        out_shape=jax.ShapeDtypeStruct((rhs, count), F32),
        in_specs=[ANY] * 4 + [VMEM],
        out_specs=VMEM,
        scratch_shapes=[
            pltpu.VMEM((rhs, count), F32),
            pltpu.VMEM((leaves, leaf, rank), BF),
            pltpu.VMEM((leaves * rank, rank), BF),
            pltpu.VMEM((rhs, leaves * rank), BF),
            pltpu.VMEM((2, rhs, rim), F32),
            dma((2 + leaves // 8,)),
            dma((2,)),
            dma((2,)),
        ],
        compiler_params=pltpu.CompilerParams(
            vmem_limit_bytes=LIMIT, collective_id=1, has_side_effects=True
        ),
        name="finish",
    )(halo, near, leaf_bases, flat_transfers, field)
    return jnp.swapaxes(out, 0, 1)[None]


def solution(mesh):
    placed = (
        P("outer", "inner", None),
        P("outer", "inner", None),
        P("outer", "inner", None),
        P("outer", "inner", None, None),
        P("outer", "inner", None, None),
        P("outer", "inner", None, None),
        P("outer", None, None, None),
        P("outer", "inner", None),
        P("outer", "inner"),
        P("outer", "inner"),
    )
    return jax.shard_map(
        on_device, mesh=mesh, in_specs=placed, out_specs=P("outer", "inner", None), check_vma=False
    )
```

```python
import functools

import jax
import jax.numpy as jnp
from jax import lax
from jax.experimental import pallas as pl
from jax.experimental.pallas import tpu as pltpu
from jax.sharding import PartitionSpec as P

REACH = 4
RIDGE = 0.25
EXTRA = 16
GROUP = 4
BF = jnp.bfloat16
F32 = jnp.float32
VMEM = pl.BlockSpec(memory_space=pltpu.VMEM)
SMEM = pl.BlockSpec(memory_space=pltpu.SMEM)
ANY = pl.BlockSpec(memory_space=pl.ANY)
MESH = pl.DeviceIdType.MESH
LIMIT = 56 * 2**20


def dot(left, right, left_dim, right_dim):
    return lax.dot_general(
        left, right, (((left_dim,), (right_dim,)), ((), ())), preferred_element_type=F32
    )


def norm_rows(block):
    wide = block.astype(F32)
    total = 0.5 * jnp.sum(wide * wide, 0, keepdims=True)
    high = total.astype(BF).astype(F32)
    rest = total - high
    middle = rest.astype(BF).astype(F32)
    parts = (high, middle, rest - middle)
    row = lax.broadcasted_iota(jnp.int32, (EXTRA, block.shape[1]), 0)
    first = jnp.where((row >= 3) & (row < 6), 1.0, 0.0)
    second = jnp.where(row < 3, 1.0, 0.0)
    for k in range(3):
        first = jnp.where(row == k, -parts[k], first)
        second = jnp.where(row == 3 + k, -parts[k], second)
    return first.astype(BF), second.astype(BF)


def columns(index, width):
    return pl.ds(pl.multiple_of(index * width, width), width)


def tile_of(points, firsts, seconds, cols_a, cols_b):
    left = jnp.concatenate([points[:, cols_a], firsts[:, cols_a]], 0)
    right = jnp.concatenate([points[:, cols_b], seconds[:, cols_b]], 0)
    return jnp.exp(dot(left, right, 0, 0)).astype(BF)


def exchange_kernel(
    inner, outer, leaves,
    pt_hbm, ct_hbm, bases_hbm, transfers_hbm, parent, couplings, group_couplings, far,
    halo_points, halo_charges, near, field_out,
    points, charges, bases, transfers, skeletons, packed, slots, group_slots, tiles,
    load_sem, halo_send, halo_recv, node_send, node_recv, group_send, group_recv,
):
    me, group = lax.axis_index("inner"), lax.axis_index("outer")
    right, left = lax.rem(me + 1, inner), lax.rem(me + inner - 1, inner)
    rhs, count = ct_hbm.shape
    leaf = count // leaves
    rim = REACH * leaf
    rank = parent.shape[1]
    chunk = 8
    loads = [
        pltpu.make_async_copy(ct_hbm, charges, load_sem.at[0]),
        pltpu.make_async_copy(transfers_hbm, transfers, load_sem.at[1]),
        pltpu.make_async_copy(pt_hbm, points, load_sem.at[2]),
    ]
    base_loads = [
        pltpu.make_async_copy(
            bases_hbm.at[pl.ds(k * chunk, chunk)], bases.at[pl.ds(k * chunk, chunk)], load_sem.at[3 + k]
        )
        for k in range(leaves // chunk)
    ]
    loads[0].start()
    for copy in base_loads:
        copy.start()
    loads[1].start()
    loads[2].start()
    barrier = pltpu.get_barrier_semaphore()
    for k in range(1, inner):
        pl.semaphore_signal(
            barrier, inc=1, device_id={"inner": lax.rem(me + k, inner)}, device_id_type=MESH
        )
    for k in range(1, outer):
        pl.semaphore_signal(
            barrier, inc=1, device_id={"outer": lax.rem(group + k, outer)}, device_id_type=MESH
        )

    loads[0].wait()
    for k, copy in enumerate(base_loads):
        copy.wait()
        for index in range(k * chunk, (k + 1) * chunk):
            block = charges[:, index * leaf : (index + 1) * leaf]
            skeletons[:, index * rank : (index + 1) * rank] = dot(block, bases[index], 1, 0).astype(BF)
    loads[1].wait()
    node = dot(skeletons[...], transfers[...], 1, 0).astype(BF)
    packed[:rhs] = node.astype(F32)
    packed[rhs:] = dot(node, parent[...], 1, 0)
    slots[me] = packed[...]

    pl.semaphore_wait(barrier, inner + outer - 2)

    def node_copy(k):
        return pltpu.make_async_remote_copy(
            src_ref=packed, dst_ref=slots.at[me], send_sem=node_send.at[k], recv_sem=node_recv.at[me],
            device_id={"inner": lax.rem(me + k, inner)}, device_id_type=MESH,
        )

    for k in range(1, inner):
        node_copy(k).start()
    halo_copies = []
    for k, (source, target, peer, begin) in enumerate((
        (pt_hbm, halo_points.at[0], right, count - rim),
        (ct_hbm, halo_charges.at[0], right, count - rim),
        (pt_hbm, halo_points.at[1], left, 0),
        (ct_hbm, halo_charges.at[1], left, 0),
    )):
        copy = pltpu.make_async_remote_copy(
            src_ref=source.at[:, pl.ds(begin, rim)], dst_ref=target,
            send_sem=halo_send.at[k], recv_sem=halo_recv.at[k],
            device_id={"inner": peer}, device_id_type=MESH,
        )
        copy.start()
        halo_copies.append(copy)
    loads[2].wait()

    def own_tile(index, slot):
        cols = columns(index, leaf)
        block = points[:, cols]
        first, second = norm_rows(block)
        left_form = jnp.concatenate([block, first], 0)
        right_form = jnp.concatenate([block, second], 0)
        tiles[slot] = jnp.exp(dot(left_form, right_form, 0, 0)).astype(BF)

    def diagonal(index, carry):
        for k in range(GROUP):
            at = index * GROUP + k
            own_tile(jnp.minimum(at + 1, leaves - 1), (k + 1) % 2)
            cols = columns(at, leaf)
            own = charges[:, cols]
            near[:, cols] = RIDGE * own.astype(F32) + dot(own, tiles[k % 2], 1, 0)
        return carry

    own_tile(0, 0)
    half = leaves // GROUP // 2
    lax.fori_loop(0, half, diagonal, 0)

    for k in range(1, inner):
        sender = lax.rem(me + k, inner)
        pltpu.make_async_copy(packed, slots.at[sender], node_recv.at[sender]).wait()
    group_slots[group] = jnp.sum(slots[:, rhs:], 0).astype(BF)

    def group_copy(k):
        return pltpu.make_async_remote_copy(
            src_ref=group_slots.at[group], dst_ref=group_slots.at[group],
            send_sem=group_send.at[k], recv_sem=group_recv.at[group],
            device_id={"outer": lax.rem(group + k, outer)}, device_id_type=MESH,
        )

    for k in range(1, outer):
        group_copy(k).start()
    field = jnp.zeros((rhs, rank), F32)
    for j in range(couplings.shape[0]):
        field += dot(slots[far[0, j], :rhs].astype(BF), couplings[j], 1, 1)
    lax.fori_loop(half, leaves // GROUP, diagonal, 0)
    group_field = jnp.zeros((rhs, rank), F32)
    for k in range(1, outer):
        sender = lax.rem(group + k, outer)
        pltpu.make_async_copy(group_slots.at[group], group_slots.at[sender], group_recv.at[sender]).wait()
        group_field += dot(group_slots[sender], group_couplings[sender], 1, 1)
    field += dot(group_field.astype(BF), parent[...], 1, 1)
    field_out[...] = field.astype(BF)
    for k in range(1, inner):
        node_copy(k).wait_send()
    for k in range(1, outer):
        group_copy(k).wait_send()
    for copy in halo_copies:
        copy.wait()


def pair_kernel(
    leaves, leaf,
    pairs, live, pt_hbm, ct_hbm, halo_points, halo_charges, near_hbm,
    out_near, out_halo,
    points, charges, firsts, seconds, totals, tiles, flipped, sem,
):
    rim = REACH * leaf
    count = leaves * leaf
    spots = (pl.ds(0, rim), pl.ds(rim + count, rim))
    own = pl.ds(rim, count)
    copies = [
        pltpu.make_async_copy(pt_hbm, points.at[:, own], sem.at[0]),
        pltpu.make_async_copy(halo_points.at[0], points.at[:, spots[0]], sem.at[1]),
        pltpu.make_async_copy(halo_points.at[1], points.at[:, spots[1]], sem.at[2]),
        pltpu.make_async_copy(ct_hbm, charges.at[:, own], sem.at[3]),
        pltpu.make_async_copy(halo_charges.at[0], charges.at[:, spots[0]], sem.at[4]),
        pltpu.make_async_copy(halo_charges.at[1], charges.at[:, spots[1]], sem.at[5]),
        pltpu.make_async_copy(near_hbm, totals.at[:, own], sem.at[6]),
    ]
    for copy in copies:
        copy.start()
    for spot in spots:
        totals[:, spot] = jnp.zeros((totals.shape[0], rim), F32)
    for copy in copies:
        copy.wait()

    def build(index, carry):
        cols = columns(index, leaf)
        firsts[:, cols], seconds[:, cols] = norm_rows(points[:, cols])
        return carry

    lax.fori_loop(0, leaves + 2 * REACH, build, 0, unroll=2)

    number = live[0, 0]

    def spans(index):
        return columns(pairs[0, index] + REACH, leaf), columns(pairs[1, index], leaf)

    def make(index, slot):
        cols_a, cols_b = spans(jnp.minimum(index, number - 1))
        tile = tile_of(points, firsts, seconds, cols_a, cols_b)
        tiles[slot] = tile
        flipped[slot] = tile.T

    def use(index, slot):
        cols_a, cols_b = spans(index)
        totals[:, cols_b] += dot(charges[:, cols_a], tiles[slot], 1, 0)
        totals[:, cols_a] += dot(charges[:, cols_b], flipped[slot], 1, 0)

    def block(index, carry):
        for k in range(GROUP):
            at = index * GROUP + k
            make(at + 1, (k + 1) % 2)
            use(at, k % 2)
        return carry

    def single(index, carry):
        make(index + 1, lax.rem(index + 1, 2))
        use(index, lax.rem(index, 2))
        return carry

    make(0, 0)
    whole = number // GROUP
    lax.fori_loop(0, whole, block, 0)
    lax.fori_loop(whole * GROUP, number, single, 0)
    writes = [
        pltpu.make_async_copy(totals.at[:, own], out_near, sem.at[0]),
        pltpu.make_async_copy(totals.at[:, spots[0]], out_halo.at[0], sem.at[1]),
        pltpu.make_async_copy(totals.at[:, spots[1]], out_halo.at[1], sem.at[2]),
    ]
    for copy in writes:
        copy.start()
    for copy in writes:
        copy.wait()


def finish_kernel(
    inner,
    halo, near_hbm, bases_hbm, transfers_hbm, field,
    out,
    near, bases, transfers, leaf_fields, arrived, load_sem, send_sem, recv_sem,
):
    me = lax.axis_index("inner")
    right, left = lax.rem(me + 1, inner), lax.rem(me + inner - 1, inner)
    leaves, leaf, rank = bases.shape
    count = near.shape[1]
    rim = REACH * leaf
    chunk = 8
    barrier = pltpu.get_barrier_semaphore()
    for peer in (left, right):
        pl.semaphore_signal(barrier, inc=1, device_id={"inner": peer}, device_id_type=MESH)
    loads = [
        pltpu.make_async_copy(transfers_hbm, transfers, load_sem.at[0]),
        pltpu.make_async_copy(near_hbm, near, load_sem.at[1]),
    ]
    base_loads = [
        pltpu.make_async_copy(
            bases_hbm.at[pl.ds(k * chunk, chunk)], bases.at[pl.ds(k * chunk, chunk)], load_sem.at[2 + k]
        )
        for k in range(leaves // chunk)
    ]
    for copy in loads + base_loads:
        copy.start()
    loads[0].wait()
    leaf_fields[...] = dot(field[...], transfers[...], 1, 1).astype(BF)
    pl.semaphore_wait(barrier, 2)
    copies = []
    for k, peer in enumerate((left, right)):
        copy = pltpu.make_async_remote_copy(
            src_ref=halo.at[k], dst_ref=arrived.at[1 - k], send_sem=send_sem.at[k],
            recv_sem=recv_sem.at[1 - k], device_id={"inner": peer}, device_id_type=MESH,
        )
        copy.start()
        copies.append(copy)
    loads[1].wait()
    for k, copy in enumerate(base_loads):
        copy.wait()
        for index in range(k * chunk, (k + 1) * chunk):
            span = slice(index * leaf, (index + 1) * leaf)
            part = leaf_fields[:, index * rank : (index + 1) * rank]
            out[:, span] = near[:, span] + dot(part, bases[index], 1, 1)
    for copy in copies:
        copy.wait()
    out[:, :rim] += arrived[0]
    out[:, count - rim :] += arrived[1]


def on_device(
    points, charges, bases, transfers, parents, couplings, group_couplings, near_pairs, pair_count, far_list
):
    leaves = transfers.shape[1]
    count = points.shape[1]
    leaf = count // leaves
    dim, rhs, rank = points.shape[2], charges.shape[2], bases.shape[2]
    rim = REACH * leaf
    wide = count + 2 * rim
    inner, outer = lax.axis_size("inner"), lax.axis_size("outer")
    pt = jnp.swapaxes(points[0], 0, 1)
    ct = jnp.swapaxes(charges[0], 0, 1)
    pairs = jnp.swapaxes(near_pairs[0], 0, 1)
    leaf_bases = bases[0].reshape(leaves, leaf, rank)
    flat_transfers = transfers[0].reshape(leaves * rank, rank)
    dma = pltpu.SemaphoreType.DMA
    halo_points, halo_charges, near, field = pl.pallas_call(
        functools.partial(exchange_kernel, inner, outer, leaves),
        out_shape=[
            jax.ShapeDtypeStruct((2, dim, rim), BF),
            jax.ShapeDtypeStruct((2, rhs, rim), BF),
            jax.ShapeDtypeStruct((rhs, count), F32),
            jax.ShapeDtypeStruct((rhs, rank), BF),
        ],
        in_specs=[ANY] * 4 + [VMEM] * 3 + [SMEM],
        out_specs=[ANY, ANY, VMEM, VMEM],
        scratch_shapes=[
            pltpu.VMEM((dim, count), BF),
            pltpu.VMEM((rhs, count), BF),
            pltpu.VMEM((leaves, leaf, rank), BF),
            pltpu.VMEM((leaves * rank, rank), BF),
            pltpu.VMEM((rhs, leaves * rank), BF),
            pltpu.VMEM((2 * rhs, rank), F32),
            pltpu.VMEM((inner, 2 * rhs, rank), F32),
            pltpu.VMEM((outer, rhs, rank), BF),
            pltpu.VMEM((2, leaf, leaf), BF),
            dma((3 + leaves // 8,)),
            dma((4,)),
            dma((4,)),
            dma((inner,)),
            dma((inner,)),
            dma((outer,)),
            dma((outer,)),
        ],
        compiler_params=pltpu.CompilerParams(
            vmem_limit_bytes=LIMIT, collective_id=0, has_side_effects=True
        ),
        name="exchange",
    )(pt, ct, leaf_bases, flat_transfers, parents[0, 0], couplings[0], group_couplings[0], far_list)
    near, halo = pl.pallas_call(
        functools.partial(pair_kernel, leaves, leaf),
        out_shape=[
            jax.ShapeDtypeStruct((rhs, count), F32),
            jax.ShapeDtypeStruct((2, rhs, rim), F32),
        ],
        in_specs=[SMEM, SMEM] + [ANY] * 5,
        out_specs=[ANY] * 2,
        scratch_shapes=[
            pltpu.VMEM((dim, wide), BF),
            pltpu.VMEM((rhs, wide), BF),
            pltpu.VMEM((EXTRA, wide), BF),
            pltpu.VMEM((EXTRA, wide), BF),
            pltpu.VMEM((rhs, wide), F32),
            pltpu.VMEM((2, leaf, leaf), BF),
            pltpu.VMEM((2, leaf, leaf), BF),
            dma((7,)),
        ],
        compiler_params=pltpu.CompilerParams(vmem_limit_bytes=LIMIT),
        name="pairs",
    )(pairs, pair_count, pt, ct, halo_points, halo_charges, near)
    out = pl.pallas_call(
        functools.partial(finish_kernel, inner),
        out_shape=jax.ShapeDtypeStruct((rhs, count), F32),
        in_specs=[ANY] * 4 + [VMEM],
        out_specs=VMEM,
        scratch_shapes=[
            pltpu.VMEM((rhs, count), F32),
            pltpu.VMEM((leaves, leaf, rank), BF),
            pltpu.VMEM((leaves * rank, rank), BF),
            pltpu.VMEM((rhs, leaves * rank), BF),
            pltpu.VMEM((2, rhs, rim), F32),
            dma((2 + leaves // 8,)),
            dma((2,)),
            dma((2,)),
        ],
        compiler_params=pltpu.CompilerParams(
            vmem_limit_bytes=LIMIT, collective_id=1, has_side_effects=True
        ),
        name="finish",
    )(halo, near, leaf_bases, flat_transfers, field)
    return jnp.swapaxes(out, 0, 1)[None]


def solution(mesh):
    placed = (
        P("outer", "inner", None),
        P("outer", "inner", None),
        P("outer", "inner", None),
        P("outer", "inner", None, None),
        P("outer", "inner", None, None),
        P("outer", "inner", None, None),
        P("outer", None, None, None),
        P("outer", "inner", None),
        P("outer", "inner"),
        P("outer", "inner"),
    )
    return jax.shard_map(
        on_device, mesh=mesh, in_specs=placed, out_specs=P("outer", "inner", None), check_vma=False
    )
```

```python
import functools

import jax
import jax.numpy as jnp
from jax import lax
from jax.experimental import pallas as pl
from jax.experimental.pallas import tpu as pltpu
from jax.sharding import PartitionSpec as P

REACH = 4
RIDGE = 0.25
EXTRA = 16
GROUP = 4
ROOTS = 2
BF = jnp.bfloat16
F32 = jnp.float32
VMEM = pl.BlockSpec(memory_space=pltpu.VMEM)
SMEM = pl.BlockSpec(memory_space=pltpu.SMEM)
ANY = pl.BlockSpec(memory_space=pl.ANY)
MESH = pl.DeviceIdType.MESH
LIMIT = 56 * 2**20


def dot(left, right, left_dim, right_dim):
    return lax.dot_general(
        left, right, (((left_dim,), (right_dim,)), ((), ())), preferred_element_type=F32
    )


def norm_rows(block):
    wide = block.astype(F32)
    total = 0.5 * jnp.sum(wide * wide, 0, keepdims=True)
    high = total.astype(BF).astype(F32)
    rest = total - high
    middle = rest.astype(BF).astype(F32)
    parts = (high, middle, rest - middle)
    row = lax.broadcasted_iota(jnp.int32, (EXTRA, block.shape[1]), 0)
    first = jnp.where((row >= 3) & (row < 6), 1.0, 0.0)
    second = jnp.where(row < 3, 1.0, 0.0)
    for k in range(3):
        first = jnp.where(row == k, -parts[k], first)
        second = jnp.where(row == 3 + k, -parts[k], second)
    return first.astype(BF), second.astype(BF)


def columns(index, width):
    return pl.ds(pl.multiple_of(index * width, width), width)


def tile_of(points, firsts, seconds, cols_a, cols_b):
    left = jnp.concatenate([points[:, cols_a], firsts[:, cols_a]], 0)
    right = jnp.concatenate([points[:, cols_b], seconds[:, cols_b]], 0)
    return jnp.exp(dot(left, right, 0, 0)).astype(BF)


def exchange_kernel(
    inner, outer, leaves,
    pt_hbm, ct_hbm, bases_hbm, transfers_hbm, parent, couplings, group_couplings, far,
    halo_points, halo_charges, near, field_out,
    points, charges, bases, transfers, skeletons, term, slots, gathered, halves, group_field, tiles,
    load_sem, halo_send, halo_recv, node_send, node_recv, term_send, term_recv,
    half_send, half_recv, field_send, field_recv,
):
    me, group = lax.axis_index("inner"), lax.axis_index("outer")
    right, left = lax.rem(me + 1, inner), lax.rem(me + inner - 1, inner)
    rhs, count = ct_hbm.shape
    leaf = count // leaves
    rim = REACH * leaf
    rank = parent.shape[1]
    chunk = 8
    rows = rhs // ROOTS
    roots = [h * (inner // ROOTS) for h in range(ROOTS)]
    is_root = functools.reduce(jnp.logical_or, [me == root for root in roots])
    peers = [lax.rem(me + k, inner) for k in range(1, inner)]
    others = [lax.rem(group + k, outer) for k in range(1, outer)]
    loads = [
        pltpu.make_async_copy(ct_hbm, charges, load_sem.at[0]),
        pltpu.make_async_copy(transfers_hbm, transfers, load_sem.at[1]),
        pltpu.make_async_copy(pt_hbm, points, load_sem.at[2]),
    ]
    base_loads = [
        pltpu.make_async_copy(
            bases_hbm.at[pl.ds(k * chunk, chunk)], bases.at[pl.ds(k * chunk, chunk)], load_sem.at[3 + k]
        )
        for k in range(leaves // chunk)
    ]
    loads[0].start()
    for copy in base_loads:
        copy.start()
    loads[1].start()
    loads[2].start()
    barrier = pltpu.get_barrier_semaphore()
    for peer in peers:
        pl.semaphore_signal(barrier, inc=1, device_id={"inner": peer}, device_id_type=MESH)

    @pl.when(is_root)
    def _():
        for other in others:
            pl.semaphore_signal(barrier, inc=1, device_id={"outer": other}, device_id_type=MESH)

    loads[0].wait()
    for k, copy in enumerate(base_loads):
        copy.wait()
        for index in range(k * chunk, (k + 1) * chunk):
            block = charges[:, index * leaf : (index + 1) * leaf]
            skeletons[:, index * rank : (index + 1) * rank] = dot(block, bases[index], 1, 0).astype(BF)
    loads[1].wait()
    node = dot(skeletons[...], transfers[...], 1, 0).astype(BF)
    slots[me] = node
    term[...] = dot(node, parent[...], 1, 0)
    gathered[me] = term[:rows]
    for h in range(1, ROOTS):

        @pl.when(me == roots[h])
        def _(h=h):
            gathered[me] = term[h * rows : (h + 1) * rows]

    @pl.when(is_root)
    def _():
        pl.semaphore_wait(barrier, inner + outer - 2)

    @pl.when(jnp.logical_not(is_root))
    def _():
        pl.semaphore_wait(barrier, inner - 1)

    def remote(source, target, send, recv, **where):
        return pltpu.make_async_remote_copy(
            src_ref=source, dst_ref=target, send_sem=send, recv_sem=recv,
            device_id=where, device_id_type=MESH,
        )

    term_copies = [
        remote(term.at[pl.ds(h * rows, rows)], gathered.at[me], term_send.at[h], term_recv.at[me], inner=root)
        for h, root in enumerate(roots)
    ]
    for root, copy in zip(roots, term_copies):
        pl.when(me != root)(copy.start)
    halo_copies = [
        remote(
            source.at[:, pl.ds(begin, rim)], target, halo_send.at[k], halo_recv.at[k], inner=peer
        )
        for k, (source, target, peer, begin) in enumerate((
            (pt_hbm, halo_points.at[0], right, count - rim),
            (pt_hbm, halo_points.at[1], left, 0),
            (ct_hbm, halo_charges.at[0], right, count - rim),
            (ct_hbm, halo_charges.at[1], left, 0),
        ))
    ]
    node_copies = [
        remote(slots.at[me], slots.at[me], node_send.at[k], node_recv.at[me], inner=peer)
        for k, peer in enumerate(peers)
    ]
    half_copies = [
        remote(halves.at[group], halves.at[group], half_send.at[k], half_recv.at[group], outer=other)
        for k, other in enumerate(others)
    ]
    field_copies = [
        [
            remote(group_field.at[h], group_field.at[h], field_send.at[k], field_recv.at[h], inner=peer)
            for k, peer in enumerate(peers)
        ]
        for h in range(ROOTS)
    ]
    for copy in halo_copies + node_copies:
        copy.start()
    loads[2].wait()
    edge = leaf // 2

    def own_tile(index, slot):
        block = points[:, columns(index, leaf)]
        first, second = norm_rows(block)
        left_form = jnp.concatenate([block, first], 0)
        right_form = jnp.concatenate([block, second], 0)
        upper = jnp.exp(dot(left_form[:, :edge], right_form, 0, 0)).astype(BF)
        tiles[slot, :edge] = upper
        tiles[slot, edge:, :edge] = upper[:, edge:].T
        tiles[slot, edge:, edge:] = jnp.exp(
            dot(left_form[:, edge:], right_form[:, edge:], 0, 0)
        ).astype(BF)

    def diagonal(index, carry):
        for k in range(GROUP):
            at = index * GROUP + k
            own_tile(jnp.minimum(at + 1, leaves - 1), (k + 1) % 2)
            cols = columns(at, leaf)
            own = charges[:, cols]
            near[:, cols] = RIDGE * own.astype(F32) + dot(own, tiles[k % 2], 1, 0)
        return carry

    own_tile(0, 0)
    total = leaves // GROUP
    stops = (3 * total // 8, 5 * total // 8)
    lax.fori_loop(0, stops[0], diagonal, 0)

    @pl.when(is_root)
    def _():
        for peer in peers:
            pltpu.make_async_copy(gathered.at[me], gathered.at[peer], term_recv.at[peer]).wait()
        halves[group] = jnp.sum(gathered[...], 0).astype(BF).astype(F32)
        for copy in half_copies:
            copy.start()

    lax.fori_loop(stops[0], stops[1], diagonal, 0)
    for h, root in enumerate(roots):

        @pl.when(me == root)
        def _(h=h):
            part = jnp.zeros((rows, rank), F32)
            for other in others:
                pltpu.make_async_copy(halves.at[group], halves.at[other], half_recv.at[other]).wait()
                part += dot(halves[other].astype(BF), group_couplings[other], 1, 1)
            group_field[h] = part.astype(BF).astype(F32)
            for copy in field_copies[h]:
                copy.start()

    lax.fori_loop(stops[1], total, diagonal, 0)
    for peer in peers:
        pltpu.make_async_copy(slots.at[me], slots.at[peer], node_recv.at[peer]).wait()
    field = jnp.zeros((rhs, rank), F32)
    for j in range(couplings.shape[0]):
        field += dot(slots[far[0, j]], couplings[j], 1, 1)
    for h, root in enumerate(roots):

        @pl.when(me != root)
        def _(h=h):
            pltpu.make_async_copy(group_field.at[h], group_field.at[h], field_recv.at[h]).wait()

    whole = jnp.concatenate([group_field[h] for h in range(ROOTS)], 0).astype(BF)
    field_out[...] = (field + dot(whole, parent[...], 1, 1)).astype(BF)
    for root, copy in zip(roots, term_copies):
        pl.when(me != root)(copy.wait_send)
    for copy in node_copies:
        copy.wait_send()
    for h, root in enumerate(roots):

        @pl.when(me == root)
        def _(h=h):
            for copy in half_copies + field_copies[h]:
                copy.wait_send()

    for copy in halo_copies:
        copy.wait()


def pair_kernel(
    leaves, leaf,
    pairs, live, pt_hbm, ct_hbm, halo_points, halo_charges,
    out_near, out_halo,
    points, charges, firsts, seconds, totals, tiles, flipped, sem,
):
    rim = REACH * leaf
    count = leaves * leaf
    chunk = 8
    spots = (pl.ds(0, rim), pl.ds(rim + count, rim))
    own = pl.ds(rim, count)
    copies = [
        pltpu.make_async_copy(halo_points.at[0], points.at[:, spots[0]], sem.at[0]),
        pltpu.make_async_copy(halo_points.at[1], points.at[:, spots[1]], sem.at[1]),
    ]
    copies += [
        pltpu.make_async_copy(
            pt_hbm.at[:, pl.ds(k * chunk * leaf, chunk * leaf)],
            points.at[:, pl.ds(rim + k * chunk * leaf, chunk * leaf)],
            sem.at[2 + k],
        )
        for k in range(leaves // chunk)
    ]
    at = len(copies)
    charge_copies = [
        pltpu.make_async_copy(ct_hbm, charges.at[:, own], sem.at[at]),
        pltpu.make_async_copy(halo_charges.at[0], charges.at[:, spots[0]], sem.at[at + 1]),
        pltpu.make_async_copy(halo_charges.at[1], charges.at[:, spots[1]], sem.at[at + 2]),
    ]
    for copy in copies + charge_copies:
        copy.start()
    totals[...] = jnp.zeros_like(totals)

    def build(index, carry):
        cols = columns(index, leaf)
        firsts[:, cols], seconds[:, cols] = norm_rows(points[:, cols])
        return carry

    spans_built = [(0, REACH), (REACH + leaves, 2 * REACH + leaves)]
    spans_built += [(REACH + k * chunk, REACH + (k + 1) * chunk) for k in range(leaves // chunk)]
    for copy, (low, high) in zip(copies, spans_built):
        copy.wait()
        lax.fori_loop(low, high, build, 0, unroll=2)
    for copy in charge_copies:
        copy.wait()
    number = live[0, 0]

    def spans(index):
        return columns(pairs[0, index] + REACH, leaf), columns(pairs[1, index], leaf)

    def make(index, slot):
        cols_a, cols_b = spans(jnp.minimum(index, number - 1))
        tile = tile_of(points, firsts, seconds, cols_a, cols_b)
        tiles[slot] = tile
        flipped[slot] = tile.T

    def use(index, slot):
        cols_a, cols_b = spans(index)
        totals[:, cols_b] += dot(charges[:, cols_a], tiles[slot], 1, 0)
        totals[:, cols_a] += dot(charges[:, cols_b], flipped[slot], 1, 0)

    def block(index, carry):
        for k in range(GROUP):
            at = index * GROUP + k
            make(at + 1, (k + 1) % 2)
            use(at, k % 2)
        return carry

    def single(index, carry):
        make(index + 1, lax.rem(index + 1, 2))
        use(index, lax.rem(index, 2))
        return carry

    make(0, 0)
    whole = number // GROUP
    lax.fori_loop(0, whole, block, 0)
    lax.fori_loop(whole * GROUP, number, single, 0)
    write = pltpu.make_async_copy(totals.at[:, own], out_near, sem.at[0])
    write.start()
    for k, spot in enumerate(spots):
        out_halo[k] = totals[:, spot].astype(BF)
    write.wait()


def finish_kernel(
    inner,
    halo, near_hbm, own_hbm, bases_hbm, transfers_hbm, field,
    out, arrived,
    near, own, bases, transfers, leaf_fields, load_sem, store_sem, send_sem, recv_sem,
):
    me = lax.axis_index("inner")
    right, left = lax.rem(me + 1, inner), lax.rem(me + inner - 1, inner)
    leaves, leaf, rank = bases.shape
    chunk = 8
    parts = leaves // chunk
    width = chunk * leaf
    barrier = pltpu.get_barrier_semaphore()
    for peer in (left, right):
        pl.semaphore_signal(barrier, inc=1, device_id={"inner": peer}, device_id_type=MESH)
    loads = [pltpu.make_async_copy(transfers_hbm, transfers, load_sem.at[0])]
    near_loads, own_loads, base_loads = [], [], []
    for k in range(parts):
        span = pl.ds(k * width, width)
        leaf_span = pl.ds(k * chunk, chunk)
        base_loads.append(
            pltpu.make_async_copy(bases_hbm.at[leaf_span], bases.at[leaf_span], load_sem.at[1 + k])
        )
        near_loads.append(
            pltpu.make_async_copy(near_hbm.at[:, span], near.at[:, span], load_sem.at[1 + parts + k])
        )
        own_loads.append(
            pltpu.make_async_copy(own_hbm.at[:, span], own.at[:, span], load_sem.at[1 + 2 * parts + k])
        )
    loads[0].start()
    for group in zip(base_loads, near_loads, own_loads):
        for copy in group:
            copy.start()
    pl.semaphore_wait(barrier, 2)
    copies = []
    for k, peer in enumerate((left, right)):
        copy = pltpu.make_async_remote_copy(
            src_ref=halo.at[k], dst_ref=arrived.at[1 - k], send_sem=send_sem.at[k],
            recv_sem=recv_sem.at[1 - k], device_id={"inner": peer}, device_id_type=MESH,
        )
        copy.start()
        copies.append(copy)
    loads[0].wait()
    leaf_fields[...] = dot(field[...], transfers[...], 1, 1).astype(BF)
    stores = []
    for k in range(parts):
        base_loads[k].wait()
        near_loads[k].wait()
        own_loads[k].wait()
        for index in range(k * chunk, (k + 1) * chunk):
            span = slice(index * leaf, (index + 1) * leaf)
            part = leaf_fields[:, index * rank : (index + 1) * rank]
            near[:, span] += own[:, span] + dot(part, bases[index], 1, 1)
        span = pl.ds(k * width, width)
        store = pltpu.make_async_copy(near.at[:, span], out.at[:, span], store_sem.at[k])
        store.start()
        stores.append(store)
    for copy in stores + copies:
        copy.wait()


def on_device(
    points, charges, bases, transfers, parents, couplings, group_couplings, near_pairs, pair_count, far_list
):
    leaves = transfers.shape[1]
    count = points.shape[1]
    leaf = count // leaves
    dim, rhs, rank = points.shape[2], charges.shape[2], bases.shape[2]
    rim = REACH * leaf
    wide = count + 2 * rim
    inner, outer = lax.axis_size("inner"), lax.axis_size("outer")
    pt = jnp.swapaxes(points[0], 0, 1)
    ct = jnp.swapaxes(charges[0], 0, 1)
    pairs = jnp.swapaxes(near_pairs[0], 0, 1)
    leaf_bases = bases[0].reshape(leaves, leaf, rank)
    flat_transfers = transfers[0].reshape(leaves * rank, rank)
    dma = pltpu.SemaphoreType.DMA
    parts = leaves // 8
    halo_points, halo_charges, own, field = pl.pallas_call(
        functools.partial(exchange_kernel, inner, outer, leaves),
        out_shape=[
            jax.ShapeDtypeStruct((2, dim, rim), BF),
            jax.ShapeDtypeStruct((2, rhs, rim), BF),
            jax.ShapeDtypeStruct((rhs, count), F32),
            jax.ShapeDtypeStruct((rhs, rank), BF),
        ],
        in_specs=[ANY] * 4 + [VMEM] * 3 + [SMEM],
        out_specs=[ANY, ANY, VMEM, VMEM],
        scratch_shapes=[
            pltpu.VMEM((dim, count), BF),
            pltpu.VMEM((rhs, count), BF),
            pltpu.VMEM((leaves, leaf, rank), BF),
            pltpu.VMEM((leaves * rank, rank), BF),
            pltpu.VMEM((rhs, leaves * rank), BF),
            pltpu.VMEM((rhs, rank), F32),
            pltpu.VMEM((inner, rhs, rank), BF),
            pltpu.VMEM((inner, rhs // ROOTS, rank), F32),
            pltpu.VMEM((outer, rhs // ROOTS, rank), F32),
            pltpu.VMEM((ROOTS, rhs // ROOTS, rank), F32),
            pltpu.VMEM((2, leaf, leaf), BF),
            dma((3 + parts,)),
            dma((4,)),
            dma((4,)),
            dma((inner,)),
            dma((inner,)),
            dma((ROOTS,)),
            dma((inner,)),
            dma((outer,)),
            dma((outer,)),
            dma((inner,)),
            dma((ROOTS,)),
        ],
        compiler_params=pltpu.CompilerParams(
            vmem_limit_bytes=LIMIT, collective_id=0, has_side_effects=True
        ),
        name="exchange",
    )(pt, ct, leaf_bases, flat_transfers, parents[0, 0], couplings[0], group_couplings[0], far_list)
    near, halo = pl.pallas_call(
        functools.partial(pair_kernel, leaves, leaf),
        out_shape=[
            jax.ShapeDtypeStruct((rhs, count), F32),
            jax.ShapeDtypeStruct((2, rhs, rim), BF),
        ],
        in_specs=[SMEM, SMEM] + [ANY] * 4,
        out_specs=[ANY, VMEM],
        scratch_shapes=[
            pltpu.VMEM((dim, wide), BF),
            pltpu.VMEM((rhs, wide), BF),
            pltpu.VMEM((EXTRA, wide), BF),
            pltpu.VMEM((EXTRA, wide), BF),
            pltpu.VMEM((rhs, wide), F32),
            pltpu.VMEM((2, leaf, leaf), BF),
            pltpu.VMEM((2, leaf, leaf), BF),
            dma((5 + parts,)),
        ],
        compiler_params=pltpu.CompilerParams(vmem_limit_bytes=LIMIT),
        name="pairs",
    )(pairs, pair_count, pt, ct, halo_points, halo_charges)
    main, arrived = pl.pallas_call(
        functools.partial(finish_kernel, inner),
        out_shape=[
            jax.ShapeDtypeStruct((rhs, count), F32),
            jax.ShapeDtypeStruct((2, rhs, rim), BF),
        ],
        in_specs=[ANY] * 5 + [VMEM],
        out_specs=[ANY, ANY],
        scratch_shapes=[
            pltpu.VMEM((rhs, count), F32),
            pltpu.VMEM((rhs, count), F32),
            pltpu.VMEM((leaves, leaf, rank), BF),
            pltpu.VMEM((leaves * rank, rank), BF),
            pltpu.VMEM((rhs, leaves * rank), BF),
            dma((1 + 3 * parts,)),
            dma((parts,)),
            dma((2,)),
            dma((2,)),
        ],
        compiler_params=pltpu.CompilerParams(
            vmem_limit_bytes=LIMIT, collective_id=1, has_side_effects=True
        ),
        name="finish",
    )(halo, near, own, leaf_bases, flat_transfers, field)
    middle = jnp.zeros((rhs, count - 2 * rim), F32)
    out = main + jnp.concatenate([arrived[0].astype(F32), middle, arrived[1].astype(F32)], 1)
    return jnp.swapaxes(out, 0, 1)[None]


def solution(mesh):
    placed = (
        P("outer", "inner", None),
        P("outer", "inner", None),
        P("outer", "inner", None),
        P("outer", "inner", None, None),
        P("outer", "inner", None, None),
        P("outer", "inner", None, None),
        P("outer", None, None, None),
        P("outer", "inner", None),
        P("outer", "inner"),
        P("outer", "inner"),
    )
    return jax.shard_map(
        on_device, mesh=mesh, in_specs=placed, out_specs=P("outer", "inner", None), check_vma=False
    )
```

```python
import functools

import jax
import jax.numpy as jnp
from jax import lax
from jax.experimental import pallas as pl
from jax.experimental.pallas import tpu as pltpu
from jax.sharding import PartitionSpec as P

REACH = 4
RIDGE = 0.25
EXTRA = 16
GROUP = 4
ROOTS = 2
BF = jnp.bfloat16
F32 = jnp.float32
VMEM = pl.BlockSpec(memory_space=pltpu.VMEM)
SMEM = pl.BlockSpec(memory_space=pltpu.SMEM)
ANY = pl.BlockSpec(memory_space=pl.ANY)
MESH = pl.DeviceIdType.MESH
LIMIT = 56 * 2**20


def dot(left, right, left_dim, right_dim):
    return lax.dot_general(
        left, right, (((left_dim,), (right_dim,)), ((), ())), preferred_element_type=F32
    )


def norm_rows(block):
    wide = block.astype(F32)
    total = 0.5 * jnp.sum(wide * wide, 0, keepdims=True)
    high = total.astype(BF).astype(F32)
    rest = total - high
    middle = rest.astype(BF).astype(F32)
    parts = (high, middle, rest - middle)
    row = lax.broadcasted_iota(jnp.int32, (EXTRA, block.shape[1]), 0)
    first = jnp.where((row >= 3) & (row < 6), 1.0, 0.0)
    second = jnp.where(row < 3, 1.0, 0.0)
    for k in range(3):
        first = jnp.where(row == k, -parts[k], first)
        second = jnp.where(row == 3 + k, -parts[k], second)
    return first.astype(BF), second.astype(BF)


def columns(index, width):
    return pl.ds(pl.multiple_of(index * width, width), width)


def tile_of(points, firsts, seconds, cols_a, cols_b):
    left = jnp.concatenate([points[:, cols_a], firsts[:, cols_a]], 0)
    right = jnp.concatenate([points[:, cols_b], seconds[:, cols_b]], 0)
    return jnp.exp(dot(left, right, 0, 0)).astype(BF)


def exchange_kernel(
    inner, outer, leaves,
    pt_hbm, ct_hbm, bases_hbm, transfers_hbm, parent_hbm, couplings_hbm, group_couplings_hbm, far,
    halo_points, halo_charges, near_hbm, field_out,
    points, charges, bases, transfers, parent, couplings, group_couplings, near,
    skeletons, term, slots, gathered, group_field, tiles,
    load_sem, near_sem, halo_send, halo_recv, node_send, node_recv, term_send, term_recv,
    field_send, field_recv,
):
    me, group = lax.axis_index("inner"), lax.axis_index("outer")
    right, left = lax.rem(me + 1, inner), lax.rem(me + inner - 1, inner)
    rhs, count = ct_hbm.shape
    leaf = count // leaves
    rim = REACH * leaf
    rank = parent.shape[1]
    chunk = 8
    rows = rhs // ROOTS
    roots = [h * (inner // ROOTS) for h in range(ROOTS)]
    is_root = functools.reduce(jnp.logical_or, [me == root for root in roots])
    peers = [lax.rem(me + k, inner) for k in range(1, inner)]
    others = [lax.rem(group + k, outer) for k in range(1, outer)]
    loads = [
        pltpu.make_async_copy(ct_hbm, charges, load_sem.at[0]),
        pltpu.make_async_copy(transfers_hbm, transfers, load_sem.at[1]),
        pltpu.make_async_copy(pt_hbm, points, load_sem.at[2]),
        pltpu.make_async_copy(parent_hbm, parent, load_sem.at[3]),
        pltpu.make_async_copy(couplings_hbm, couplings, load_sem.at[4]),
        pltpu.make_async_copy(group_couplings_hbm, group_couplings, load_sem.at[5]),
    ]
    base_loads = [
        pltpu.make_async_copy(
            bases_hbm.at[pl.ds(k * chunk, chunk)], bases.at[pl.ds(k * chunk, chunk)], load_sem.at[6 + k]
        )
        for k in range(leaves // chunk)
    ]
    loads[0].start()
    for copy in base_loads:
        copy.start()
    for k in (1, 3, 2, 4, 5):
        loads[k].start()
    barrier = pltpu.get_barrier_semaphore()
    for peer in peers:
        pl.semaphore_signal(barrier, inc=1, device_id={"inner": peer}, device_id_type=MESH)

    @pl.when(is_root)
    def _():
        def greet(index, carry):
            for other in others:
                pl.semaphore_signal(
                    barrier, inc=1, device_id={"inner": index, "outer": other}, device_id_type=MESH
                )
            return carry

        lax.fori_loop(0, inner, greet, 0)

    loads[0].wait()
    for k, copy in enumerate(base_loads):
        copy.wait()
        for index in range(k * chunk, (k + 1) * chunk):
            block = charges[:, index * leaf : (index + 1) * leaf]
            skeletons[:, index * rank : (index + 1) * rank] = dot(block, bases[index], 1, 0).astype(BF)
    loads[1].wait()
    node = dot(skeletons[...], transfers[...], 1, 0).astype(BF)
    slots[me] = node
    loads[3].wait()
    term[...] = dot(node, parent[...], 1, 0)
    pl.semaphore_wait(barrier, inner - 1 + ROOTS * (outer - 1))

    def remote(source, target, send, recv, **where):
        return pltpu.make_async_remote_copy(
            src_ref=source, dst_ref=target, send_sem=send, recv_sem=recv,
            device_id=where, device_id_type=MESH,
        )

    mine = group * inner + me
    term_copies = [
        remote(
            term.at[pl.ds(h * rows, rows)], gathered.at[mine],
            term_send.at[h * outer + k], term_recv.at[mine], inner=root, outer=other,
        )
        for h, root in enumerate(roots)
        for k, other in enumerate(others)
    ]
    for copy in term_copies:
        copy.start()
    halo_copies = [
        remote(
            source.at[:, pl.ds(begin, rim)], target, halo_send.at[k], halo_recv.at[k], inner=peer
        )
        for k, (source, target, peer, begin) in enumerate((
            (pt_hbm, halo_points.at[0], right, count - rim),
            (pt_hbm, halo_points.at[1], left, 0),
            (ct_hbm, halo_charges.at[0], right, count - rim),
            (ct_hbm, halo_charges.at[1], left, 0),
        ))
    ]
    node_copies = [
        remote(slots.at[me], slots.at[me], node_send.at[k], node_recv.at[me], inner=peer)
        for k, peer in enumerate(peers)
    ]
    field_copies = [
        [
            remote(group_field.at[h], group_field.at[h], field_send.at[k], field_recv.at[h], inner=peer)
            for k, peer in enumerate(peers)
        ]
        for h in range(ROOTS)
    ]
    for copy in halo_copies + node_copies:
        copy.start()
    loads[2].wait()
    edge = leaf // 2

    def own_tile(index, slot):
        block = points[:, columns(index, leaf)]
        first, second = norm_rows(block)
        left_form = jnp.concatenate([block, first], 0)
        right_form = jnp.concatenate([block, second], 0)
        upper = jnp.exp(dot(left_form[:, :edge], right_form, 0, 0)).astype(BF)
        tiles[slot, :edge] = upper
        tiles[slot, edge:, :edge] = upper[:, edge:].T
        tiles[slot, edge:, edge:] = jnp.exp(
            dot(left_form[:, edge:], right_form[:, edge:], 0, 0)
        ).astype(BF)

    def diagonal(index, carry):
        for k in range(GROUP):
            at = index * GROUP + k
            own_tile(jnp.minimum(at + 1, leaves - 1), (k + 1) % 2)
            cols = columns(at, leaf)
            own = charges[:, cols]
            near[:, cols] = RIDGE * own.astype(F32) + dot(own, tiles[k % 2], 1, 0)
        return carry

    own_tile(0, 0)
    total = leaves // GROUP
    stop = 5 * total // 8
    lax.fori_loop(0, stop, diagonal, 0)
    spans = [pl.ds(0, stop * GROUP * leaf), pl.ds(stop * GROUP * leaf, (total - stop) * GROUP * leaf)]
    near_copies = [
        pltpu.make_async_copy(near.at[:, span], near_hbm.at[:, span], near_sem.at[k])
        for k, span in enumerate(spans)
    ]
    near_copies[0].start()
    loads[4].wait()
    loads[5].wait()
    for h, root in enumerate(roots):

        @pl.when(me == root)
        def _(h=h):
            part = jnp.zeros((rows, rank), F32)
            for other in others:

                def arrive(index, carry):
                    sender = other * inner + index
                    pltpu.make_async_copy(gathered.at[mine], gathered.at[sender], term_recv.at[sender]).wait()
                    return carry

                lax.fori_loop(0, inner, arrive, 0)
                skeleton = jnp.sum(gathered[pl.ds(other * inner, inner)], 0).astype(BF)
                part += dot(skeleton, group_couplings[other], 1, 1)
            group_field[h] = part.astype(BF).astype(F32)
            for copy in field_copies[h]:
                copy.start()

    lax.fori_loop(stop, total, diagonal, 0)
    near_copies[1].start()
    for peer in peers:
        pltpu.make_async_copy(slots.at[me], slots.at[peer], node_recv.at[peer]).wait()
    field = jnp.zeros((rhs, rank), F32)
    for j in range(couplings.shape[0]):
        field += dot(slots[far[0, j]], couplings[j], 1, 1)
    for h, root in enumerate(roots):

        @pl.when(me != root)
        def _(h=h):
            pltpu.make_async_copy(group_field.at[h], group_field.at[h], field_recv.at[h]).wait()

    whole = jnp.concatenate([group_field[h] for h in range(ROOTS)], 0).astype(BF)
    field_out[...] = (field + dot(whole, parent[...], 1, 1)).astype(BF)
    for copy in term_copies + node_copies:
        copy.wait_send()
    for h, root in enumerate(roots):

        @pl.when(me == root)
        def _(h=h):
            for copy in field_copies[h]:
                copy.wait_send()

    for copy in near_copies:
        copy.wait()
    for copy in halo_copies:
        copy.wait()


def pair_kernel(
    leaves, leaf,
    pairs, live, pt_hbm, ct_hbm, halo_points, halo_charges,
    out_near, out_halo,
    points, charges, firsts, seconds, totals, tiles, flipped, halo, sem,
):
    rim = REACH * leaf
    count = leaves * leaf
    chunk = 8
    spots = (pl.ds(0, rim), pl.ds(rim + count, rim))
    own = pl.ds(rim, count)
    copies = [
        pltpu.make_async_copy(halo_points.at[0], points.at[:, spots[0]], sem.at[0]),
        pltpu.make_async_copy(halo_points.at[1], points.at[:, spots[1]], sem.at[1]),
    ]
    copies += [
        pltpu.make_async_copy(
            pt_hbm.at[:, pl.ds(k * chunk * leaf, chunk * leaf)],
            points.at[:, pl.ds(rim + k * chunk * leaf, chunk * leaf)],
            sem.at[2 + k],
        )
        for k in range(leaves // chunk)
    ]
    at = len(copies)
    charge_copies = [
        pltpu.make_async_copy(ct_hbm, charges.at[:, own], sem.at[at]),
        pltpu.make_async_copy(halo_charges.at[0], charges.at[:, spots[0]], sem.at[at + 1]),
        pltpu.make_async_copy(halo_charges.at[1], charges.at[:, spots[1]], sem.at[at + 2]),
    ]
    for copy in copies + charge_copies:
        copy.start()
    totals[...] = jnp.zeros_like(totals)

    def build(index, carry):
        cols = columns(index, leaf)
        firsts[:, cols], seconds[:, cols] = norm_rows(points[:, cols])
        return carry

    spans_built = [(0, REACH), (REACH + leaves, 2 * REACH + leaves)]
    spans_built += [(REACH + k * chunk, REACH + (k + 1) * chunk) for k in range(leaves // chunk)]
    for copy, (low, high) in zip(copies, spans_built):
        copy.wait()
        lax.fori_loop(low, high, build, 0, unroll=2)
    for copy in charge_copies:
        copy.wait()
    number = live[0, 0]

    def spans(index):
        return columns(pairs[0, index] + REACH, leaf), columns(pairs[1, index], leaf)

    def make(index, slot):
        cols_a, cols_b = spans(jnp.minimum(index, number - 1))
        tile = tile_of(points, firsts, seconds, cols_a, cols_b)
        tiles[slot] = tile
        flipped[slot] = tile.T

    def use(index, slot):
        cols_a, cols_b = spans(index)
        totals[:, cols_b] += dot(charges[:, cols_a], tiles[slot], 1, 0)
        totals[:, cols_a] += dot(charges[:, cols_b], flipped[slot], 1, 0)

    def block(index, carry):
        for k in range(GROUP):
            at = index * GROUP + k
            make(at + 1, (k + 1) % 2)
            use(at, k % 2)
        return carry

    def single(index, carry):
        make(index + 1, lax.rem(index + 1, 2))
        use(index, lax.rem(index, 2))
        return carry

    make(0, 0)
    whole = number // GROUP
    lax.fori_loop(0, whole, block, 0)
    lax.fori_loop(whole * GROUP, number, single, 0)
    write = pltpu.make_async_copy(totals.at[:, own], out_near, sem.at[0])
    write.start()
    for k, spot in enumerate(spots):
        halo[k] = totals[:, spot].astype(BF)
    halo_write = pltpu.make_async_copy(halo, out_halo, sem.at[1])
    halo_write.start()
    halo_write.wait()
    write.wait()


def finish_kernel(
    inner,
    halo, near_hbm, own_hbm, bases_hbm, transfers_hbm, field_hbm,
    out, arrived,
    near, own, bases, transfers, field, leaf_fields, load_sem, store_sem, send_sem, recv_sem,
):
    me = lax.axis_index("inner")
    right, left = lax.rem(me + 1, inner), lax.rem(me + inner - 1, inner)
    leaves, leaf, rank = bases.shape
    chunk = 8
    parts = leaves // chunk
    width = chunk * leaf
    barrier = pltpu.get_barrier_semaphore()
    for peer in (left, right):
        pl.semaphore_signal(barrier, inc=1, device_id={"inner": peer}, device_id_type=MESH)
    loads = [
        pltpu.make_async_copy(transfers_hbm, transfers, load_sem.at[0]),
        pltpu.make_async_copy(field_hbm, field, load_sem.at[1 + 3 * (leaves // chunk)]),
    ]
    near_loads, own_loads, base_loads = [], [], []
    for k in range(parts):
        span = pl.ds(k * width, width)
        leaf_span = pl.ds(k * chunk, chunk)
        base_loads.append(
            pltpu.make_async_copy(bases_hbm.at[leaf_span], bases.at[leaf_span], load_sem.at[1 + k])
        )
        near_loads.append(
            pltpu.make_async_copy(near_hbm.at[:, span], near.at[:, span], load_sem.at[1 + parts + k])
        )
        own_loads.append(
            pltpu.make_async_copy(own_hbm.at[:, span], own.at[:, span], load_sem.at[1 + 2 * parts + k])
        )
    for copy in loads:
        copy.start()
    for group in zip(base_loads, near_loads, own_loads):
        for copy in group:
            copy.start()
    pl.semaphore_wait(barrier, 2)
    copies = []
    for k, peer in enumerate((left, right)):
        copy = pltpu.make_async_remote_copy(
            src_ref=halo.at[k], dst_ref=arrived.at[1 - k], send_sem=send_sem.at[k],
            recv_sem=recv_sem.at[1 - k], device_id={"inner": peer}, device_id_type=MESH,
        )
        copy.start()
        copies.append(copy)
    for copy in loads:
        copy.wait()
    leaf_fields[...] = dot(field[...], transfers[...], 1, 1).astype(BF)
    stores = []
    for k in range(parts):
        base_loads[k].wait()
        near_loads[k].wait()
        own_loads[k].wait()
        for index in range(k * chunk, (k + 1) * chunk):
            span = slice(index * leaf, (index + 1) * leaf)
            part = leaf_fields[:, index * rank : (index + 1) * rank]
            near[:, span] += own[:, span] + dot(part, bases[index], 1, 1)
        span = pl.ds(k * width, width)
        store = pltpu.make_async_copy(near.at[:, span], out.at[:, span], store_sem.at[k])
        store.start()
        stores.append(store)
    for copy in stores + copies:
        copy.wait()


def rim_kernel(steps, main, arrived, out):
    rim = arrived.shape[2]
    out[...] = main[...]

    @pl.when(pl.program_id(0) == 0)
    def _():
        out[:, :rim] += arrived[0].astype(F32)

    @pl.when(pl.program_id(0) == steps - 1)
    def _():
        out[:, out.shape[1] - rim :] += arrived[1].astype(F32)


def on_device(
    points, charges, bases, transfers, parents, couplings, group_couplings, near_pairs, pair_count, far_list
):
    leaves = transfers.shape[1]
    count = points.shape[1]
    leaf = count // leaves
    dim, rhs, rank = points.shape[2], charges.shape[2], bases.shape[2]
    rim = REACH * leaf
    wide = count + 2 * rim
    inner, outer = lax.axis_size("inner"), lax.axis_size("outer")
    pt = jnp.swapaxes(points[0], 0, 1)
    ct = jnp.swapaxes(charges[0], 0, 1)
    pairs = jnp.swapaxes(near_pairs[0], 0, 1)
    leaf_bases = bases[0].reshape(leaves, leaf, rank)
    flat_transfers = transfers[0].reshape(leaves * rank, rank)
    dma = pltpu.SemaphoreType.DMA
    parts = leaves // 8
    halo_points, halo_charges, own, field = pl.pallas_call(
        functools.partial(exchange_kernel, inner, outer, leaves),
        out_shape=[
            jax.ShapeDtypeStruct((2, dim, rim), BF),
            jax.ShapeDtypeStruct((2, rhs, rim), BF),
            jax.ShapeDtypeStruct((rhs, count), F32),
            jax.ShapeDtypeStruct((rhs, rank), BF),
        ],
        in_specs=[ANY] * 7 + [SMEM],
        out_specs=[ANY, ANY, ANY, VMEM],
        scratch_shapes=[
            pltpu.VMEM((dim, count), BF),
            pltpu.VMEM((rhs, count), BF),
            pltpu.VMEM((leaves, leaf, rank), BF),
            pltpu.VMEM((leaves * rank, rank), BF),
            pltpu.VMEM((rank, rank), BF),
            pltpu.VMEM(couplings.shape[1:], BF),
            pltpu.VMEM(group_couplings.shape[1:], BF),
            pltpu.VMEM((rhs, count), F32),
            pltpu.VMEM((rhs, leaves * rank), BF),
            pltpu.VMEM((rhs, rank), F32),
            pltpu.VMEM((inner, rhs, rank), BF),
            pltpu.VMEM((outer * inner, rhs // ROOTS, rank), F32),
            pltpu.VMEM((ROOTS, rhs // ROOTS, rank), F32),
            pltpu.VMEM((2, leaf, leaf), BF),
            dma((6 + parts,)),
            dma((2,)),
            dma((4,)),
            dma((4,)),
            dma((inner,)),
            dma((inner,)),
            dma((ROOTS * outer,)),
            dma((outer * inner,)),
            dma((inner,)),
            dma((ROOTS,)),
        ],
        compiler_params=pltpu.CompilerParams(
            vmem_limit_bytes=LIMIT, collective_id=0, has_side_effects=True
        ),
        name="exchange",
    )(pt, ct, leaf_bases, flat_transfers, parents[0, 0], couplings[0], group_couplings[0], far_list)
    near, halo = pl.pallas_call(
        functools.partial(pair_kernel, leaves, leaf),
        out_shape=[
            jax.ShapeDtypeStruct((rhs, count), F32),
            jax.ShapeDtypeStruct((2, rhs, rim), BF),
        ],
        in_specs=[SMEM, SMEM] + [ANY] * 4,
        out_specs=[ANY, ANY],
        scratch_shapes=[
            pltpu.VMEM((dim, wide), BF),
            pltpu.VMEM((rhs, wide), BF),
            pltpu.VMEM((EXTRA, wide), BF),
            pltpu.VMEM((EXTRA, wide), BF),
            pltpu.VMEM((rhs, wide), F32),
            pltpu.VMEM((2, leaf, leaf), BF),
            pltpu.VMEM((2, leaf, leaf), BF),
            pltpu.VMEM((2, rhs, rim), BF),
            dma((5 + parts,)),
        ],
        compiler_params=pltpu.CompilerParams(vmem_limit_bytes=LIMIT),
        name="pairs",
    )(pairs, pair_count, pt, ct, halo_points, halo_charges)
    main, arrived = pl.pallas_call(
        functools.partial(finish_kernel, inner),
        out_shape=[
            jax.ShapeDtypeStruct((rhs, count), F32),
            jax.ShapeDtypeStruct((2, rhs, rim), BF),
        ],
        in_specs=[ANY] * 6,
        out_specs=[ANY, ANY],
        scratch_shapes=[
            pltpu.VMEM((rhs, count), F32),
            pltpu.VMEM((rhs, count), F32),
            pltpu.VMEM((leaves, leaf, rank), BF),
            pltpu.VMEM((leaves * rank, rank), BF),
            pltpu.VMEM((rhs, rank), BF),
            pltpu.VMEM((rhs, leaves * rank), BF),
            dma((2 + 3 * parts,)),
            dma((parts,)),
            dma((2,)),
            dma((2,)),
        ],
        compiler_params=pltpu.CompilerParams(
            vmem_limit_bytes=LIMIT, collective_id=1, has_side_effects=True
        ),
        name="finish",
    )(halo, near, own, leaf_bases, flat_transfers, field)
    steps = 4
    width = count // steps
    out = pl.pallas_call(
        functools.partial(rim_kernel, steps),
        out_shape=jax.ShapeDtypeStruct((rhs, count), F32),
        grid=(steps,),
        in_specs=[
            pl.BlockSpec((rhs, width), lambda i: (0, i)),
            pl.BlockSpec((2, rhs, rim), lambda i: (0, 0, 0)),
        ],
        out_specs=pl.BlockSpec((rhs, width), lambda i: (0, i)),
        compiler_params=pltpu.CompilerParams(vmem_limit_bytes=LIMIT),
        name="rims",
    )(main, arrived)
    return jnp.swapaxes(out, 0, 1)[None]


def solution(mesh):
    placed = (
        P("outer", "inner", None),
        P("outer", "inner", None),
        P("outer", "inner", None),
        P("outer", "inner", None, None),
        P("outer", "inner", None, None),
        P("outer", "inner", None, None),
        P("outer", None, None, None),
        P("outer", "inner", None),
        P("outer", "inner"),
        P("outer", "inner"),
    )
    return jax.shard_map(
        on_device, mesh=mesh, in_specs=placed, out_specs=P("outer", "inner", None), check_vma=False
    )
```

```python
import functools

import jax
import jax.numpy as jnp
from jax import lax
from jax.experimental import pallas as pl
from jax.experimental.pallas import tpu as pltpu
from jax.sharding import PartitionSpec as P

REACH = 4
RIDGE = 0.25
EXTRA = 16
GROUP = 4
PAIR_GROUPS = (8, 4, 1)
BF = jnp.bfloat16
F32 = jnp.float32
VMEM = pl.BlockSpec(memory_space=pltpu.VMEM)
SMEM = pl.BlockSpec(memory_space=pltpu.SMEM)
ANY = pl.BlockSpec(memory_space=pl.ANY)
MESH = pl.DeviceIdType.MESH
LIMIT = 56 * 2**20


def dot(left, right, left_dim, right_dim):
    return lax.dot_general(
        left, right, (((left_dim,), (right_dim,)), ((), ())), preferred_element_type=F32
    )


def norm_rows(block):
    wide = block.astype(F32)
    total = 0.5 * jnp.sum(wide * wide, 0, keepdims=True)
    high = total.astype(BF).astype(F32)
    rest = total - high
    middle = rest.astype(BF).astype(F32)
    parts = (high, middle, rest - middle)
    row = lax.broadcasted_iota(jnp.int32, (EXTRA, block.shape[1]), 0)
    first = jnp.where((row >= 3) & (row < 6), 1.0, 0.0)
    second = jnp.where(row < 3, 1.0, 0.0)
    for k in range(3):
        first = jnp.where(row == k, -parts[k], first)
        second = jnp.where(row == 3 + k, -parts[k], second)
    return first.astype(BF), second.astype(BF)


def columns(index, width):
    return pl.ds(pl.multiple_of(index * width, width), width)


def tile_of(points, firsts, seconds, cols_a, cols_b):
    left = jnp.concatenate([points[:, cols_a], firsts[:, cols_a]], 0)
    right = jnp.concatenate([points[:, cols_b], seconds[:, cols_b]], 0)
    return jnp.exp(dot(left, right, 0, 0)).astype(BF)


def exchange_kernel(
    inner, outer, leaves,
    pt_hbm, ct_hbm, bases_hbm, transfers_hbm, parent_hbm, couplings_hbm, group_couplings_hbm, far,
    halo_points, halo_charges, near_hbm, field_out,
    points, charges, bases, transfers, parent, couplings, group_couplings, near,
    skeletons, term, slots, gathered, parts, tiles,
    load_sem, near_sem, halo_send, halo_recv, node_send, node_recv, term_send, term_recv,
    field_send, field_recv,
):
    me, group = lax.axis_index("inner"), lax.axis_index("outer")
    right, left = lax.rem(me + 1, inner), lax.rem(me + inner - 1, inner)
    rhs, count = ct_hbm.shape
    leaf = count // leaves
    rim = REACH * leaf
    rank = parent.shape[1]
    chunk = 8
    roots = [k * (inner // outer + 2) % inner for k in range(outer - 1)]
    peers = [lax.rem(me + k, inner) for k in range(1, inner)]
    sources = [lax.rem(group + k, outer) for k in range(1, outer)]
    sinks = [lax.rem(group + outer - k, outer) for k in range(1, outer)]
    loads = [
        pltpu.make_async_copy(ct_hbm, charges, load_sem.at[0]),
        pltpu.make_async_copy(transfers_hbm, transfers, load_sem.at[1]),
        pltpu.make_async_copy(pt_hbm, points, load_sem.at[2]),
        pltpu.make_async_copy(parent_hbm, parent, load_sem.at[3]),
        pltpu.make_async_copy(couplings_hbm, couplings, load_sem.at[4]),
        pltpu.make_async_copy(group_couplings_hbm, group_couplings, load_sem.at[5]),
    ]
    base_loads = [
        pltpu.make_async_copy(
            bases_hbm.at[pl.ds(k * chunk, chunk)], bases.at[pl.ds(k * chunk, chunk)], load_sem.at[6 + k]
        )
        for k in range(leaves // chunk)
    ]
    loads[0].start()
    for copy in base_loads:
        copy.start()
    for k in (1, 3, 2, 4, 5):
        loads[k].start()
    barrier = pltpu.get_barrier_semaphore()
    for root, source in zip(roots, sources):

        @pl.when(me == root)
        def _(source=source):
            def greet(index, carry):
                pl.semaphore_signal(
                    barrier, inc=1, device_id={"inner": index, "outer": source}, device_id_type=MESH
                )
                return carry

            lax.fori_loop(0, inner, greet, 0)

    for peer in peers:
        pl.semaphore_signal(barrier, inc=1, device_id={"inner": peer}, device_id_type=MESH)

    loads[0].wait()
    for k, copy in enumerate(base_loads):
        copy.wait()
        for index in range(k * chunk, (k + 1) * chunk):
            block = charges[:, index * leaf : (index + 1) * leaf]
            skeletons[:, index * rank : (index + 1) * rank] = dot(block, bases[index], 1, 0).astype(BF)
    loads[1].wait()
    node = dot(skeletons[...], transfers[...], 1, 0).astype(BF)
    slots[me] = node
    loads[3].wait()
    term[...] = dot(node, parent[...], 1, 0)
    pl.semaphore_wait(barrier, inner - 1 + outer - 1)

    def remote(source, target, send, recv, **where):
        return pltpu.make_async_remote_copy(
            src_ref=source, dst_ref=target, send_sem=send, recv_sem=recv,
            device_id=where, device_id_type=MESH,
        )

    term_copies = [
        remote(term, gathered.at[me], term_send.at[k], term_recv.at[me], inner=root, outer=sink)
        for k, (root, sink) in enumerate(zip(roots, sinks))
    ]
    for copy in term_copies:
        copy.start()
    halo_copies = [
        remote(
            source.at[:, pl.ds(begin, rim)], target, halo_send.at[k], halo_recv.at[k], inner=peer
        )
        for k, (source, target, peer, begin) in enumerate((
            (pt_hbm, halo_points.at[0], right, count - rim),
            (pt_hbm, halo_points.at[1], left, 0),
            (ct_hbm, halo_charges.at[0], right, count - rim),
            (ct_hbm, halo_charges.at[1], left, 0),
        ))
    ]
    node_copies = [
        remote(slots.at[me], slots.at[me], node_send.at[k], node_recv.at[me], inner=peer)
        for k, peer in enumerate(peers)
    ]
    field_copies = [
        [
            remote(parts.at[h], parts.at[h], field_send.at[k], field_recv.at[h], inner=peer)
            for k, peer in enumerate(peers)
        ]
        for h in range(outer - 1)
    ]
    for copy in halo_copies + node_copies:
        copy.start()
    loads[2].wait()
    edge = leaf // 2

    def own_tile(index, slot):
        block = points[:, columns(index, leaf)]
        first, second = norm_rows(block)
        left_form = jnp.concatenate([block, first], 0)
        right_form = jnp.concatenate([block, second], 0)
        upper = jnp.exp(dot(left_form[:, :edge], right_form, 0, 0)).astype(BF)
        tiles[slot, :edge] = upper
        tiles[slot, edge:, :edge] = upper[:, edge:].T
        tiles[slot, edge:, edge:] = jnp.exp(
            dot(left_form[:, edge:], right_form[:, edge:], 0, 0)
        ).astype(BF)

    def diagonal(index, carry):
        for k in range(GROUP):
            at = index * GROUP + k
            own_tile(jnp.minimum(at + 1, leaves - 1), (k + 1) % 2)
            cols = columns(at, leaf)
            own = charges[:, cols]
            near[:, cols] = RIDGE * own.astype(F32) + dot(own, tiles[k % 2], 1, 0)
        return carry

    own_tile(0, 0)
    total = leaves // GROUP
    stop = 5 * total // 8
    lax.fori_loop(0, stop, diagonal, 0)
    spans = [pl.ds(0, stop * GROUP * leaf), pl.ds(stop * GROUP * leaf, (total - stop) * GROUP * leaf)]
    near_copies = [
        pltpu.make_async_copy(near.at[:, span], near_hbm.at[:, span], near_sem.at[k])
        for k, span in enumerate(spans)
    ]
    near_copies[0].start()
    loads[4].wait()
    loads[5].wait()
    for h, root in enumerate(roots):

        @pl.when(me == root)
        def _(h=h):
            def arrive(index, carry):
                pltpu.make_async_copy(term, gathered.at[index], term_recv.at[index]).wait()
                return carry

            lax.fori_loop(0, inner, arrive, 0)
            skeleton = jnp.sum(gathered[...], 0).astype(BF)
            parts[h] = dot(skeleton, group_couplings[sources[h]], 1, 1)
            for copy in field_copies[h]:
                copy.start()

    lax.fori_loop(stop, total, diagonal, 0)
    near_copies[1].start()
    for peer in peers:
        pltpu.make_async_copy(slots.at[me], slots.at[peer], node_recv.at[peer]).wait()
    field = jnp.zeros((rhs, rank), F32)
    for j in range(couplings.shape[0]):
        field += dot(slots[far[0, j]], couplings[j], 1, 1)
    for h, root in enumerate(roots):

        @pl.when(me != root)
        def _(h=h):
            pltpu.make_async_copy(parts.at[h], parts.at[h], field_recv.at[h]).wait()

    group_field = jnp.sum(parts[...], 0).astype(BF)
    field_out[...] = (field + dot(group_field, parent[...], 1, 1)).astype(BF)
    for copy in term_copies + node_copies:
        copy.wait_send()
    for h, root in enumerate(roots):

        @pl.when(me == root)
        def _(h=h):
            for copy in field_copies[h]:
                copy.wait_send()

    for copy in near_copies:
        copy.wait()
    for copy in halo_copies:
        copy.wait()


def pair_kernel(
    leaves, leaf,
    pairs, live, pt_hbm, ct_hbm, halo_points, halo_charges,
    out_near, out_halo,
    points, charges, firsts, seconds, totals, tiles, flipped, halo, sem,
):
    rim = REACH * leaf
    count = leaves * leaf
    chunk = 8
    spots = (pl.ds(0, rim), pl.ds(rim + count, rim))
    own = pl.ds(rim, count)
    copies = [
        pltpu.make_async_copy(halo_points.at[0], points.at[:, spots[0]], sem.at[0]),
        pltpu.make_async_copy(halo_points.at[1], points.at[:, spots[1]], sem.at[1]),
    ]
    copies += [
        pltpu.make_async_copy(
            pt_hbm.at[:, pl.ds(k * chunk * leaf, chunk * leaf)],
            points.at[:, pl.ds(rim + k * chunk * leaf, chunk * leaf)],
            sem.at[2 + k],
        )
        for k in range(leaves // chunk)
    ]
    at = len(copies)
    charge_copies = [
        pltpu.make_async_copy(ct_hbm, charges.at[:, own], sem.at[at]),
        pltpu.make_async_copy(halo_charges.at[0], charges.at[:, spots[0]], sem.at[at + 1]),
        pltpu.make_async_copy(halo_charges.at[1], charges.at[:, spots[1]], sem.at[at + 2]),
    ]
    for copy in copies + charge_copies:
        copy.start()
    totals[...] = jnp.zeros_like(totals)

    def build(index, carry):
        cols = columns(index, leaf)
        firsts[:, cols], seconds[:, cols] = norm_rows(points[:, cols])
        return carry

    spans_built = [(0, REACH), (REACH + leaves, 2 * REACH + leaves)]
    spans_built += [(REACH + k * chunk, REACH + (k + 1) * chunk) for k in range(leaves // chunk)]
    for copy, (low, high) in zip(copies, spans_built):
        copy.wait()
        lax.fori_loop(low, high, build, 0, unroll=2)
    for copy in charge_copies:
        copy.wait()
    number = live[0, 0]

    def spans(index):
        return columns(pairs[0, index] + REACH, leaf), columns(pairs[1, index], leaf)

    def make(index, slot):
        cols_a, cols_b = spans(jnp.minimum(index, number - 1))
        tile = tile_of(points, firsts, seconds, cols_a, cols_b)
        tiles[slot] = tile
        flipped[slot] = tile.T

    def use(index, slot):
        cols_a, cols_b = spans(index)
        totals[:, cols_b] += dot(charges[:, cols_a], tiles[slot], 1, 0)
        totals[:, cols_a] += dot(charges[:, cols_b], flipped[slot], 1, 0)

    make(0, 0)
    done = 0
    for size in PAIR_GROUPS:

        def block(index, carry, size=size, done=done):
            for k in range(size):
                at = done + index * size + k
                slot = k % 2 if size > 1 else lax.rem(at, 2)
                make(at + 1, 1 - slot)
                use(at, slot)
            return carry

        blocks = (number - done) // size
        lax.fori_loop(0, blocks, block, 0)
        done += blocks * size
    write = pltpu.make_async_copy(totals.at[:, own], out_near, sem.at[0])
    write.start()
    for k, spot in enumerate(spots):
        halo[k] = totals[:, spot].astype(BF)
    halo_write = pltpu.make_async_copy(halo, out_halo, sem.at[1])
    halo_write.start()
    halo_write.wait()
    write.wait()


def finish_kernel(
    inner,
    halo, near_hbm, own_hbm, bases_hbm, transfers_hbm, field_hbm,
    out, arrived,
    near, own, bases, transfers, field, leaf_fields, load_sem, store_sem, send_sem, recv_sem,
):
    me = lax.axis_index("inner")
    right, left = lax.rem(me + 1, inner), lax.rem(me + inner - 1, inner)
    leaves, leaf, rank = bases.shape
    chunk = 8
    parts = leaves // chunk
    width = chunk * leaf
    barrier = pltpu.get_barrier_semaphore()
    for peer in (left, right):
        pl.semaphore_signal(barrier, inc=1, device_id={"inner": peer}, device_id_type=MESH)
    loads = [
        pltpu.make_async_copy(transfers_hbm, transfers, load_sem.at[0]),
        pltpu.make_async_copy(field_hbm, field, load_sem.at[1 + 3 * (leaves // chunk)]),
    ]
    near_loads, own_loads, base_loads = [], [], []
    for k in range(parts):
        span = pl.ds(k * width, width)
        leaf_span = pl.ds(k * chunk, chunk)
        base_loads.append(
            pltpu.make_async_copy(bases_hbm.at[leaf_span], bases.at[leaf_span], load_sem.at[1 + k])
        )
        near_loads.append(
            pltpu.make_async_copy(near_hbm.at[:, span], near.at[:, span], load_sem.at[1 + parts + k])
        )
        own_loads.append(
            pltpu.make_async_copy(own_hbm.at[:, span], own.at[:, span], load_sem.at[1 + 2 * parts + k])
        )
    for copy in loads:
        copy.start()
    for group in zip(base_loads, near_loads, own_loads):
        for copy in group:
            copy.start()
    pl.semaphore_wait(barrier, 2)
    copies = []
    for k, peer in enumerate((left, right)):
        copy = pltpu.make_async_remote_copy(
            src_ref=halo.at[k], dst_ref=arrived.at[1 - k], send_sem=send_sem.at[k],
            recv_sem=recv_sem.at[1 - k], device_id={"inner": peer}, device_id_type=MESH,
        )
        copy.start()
        copies.append(copy)
    for copy in loads:
        copy.wait()
    leaf_fields[...] = dot(field[...], transfers[...], 1, 1).astype(BF)
    stores = []
    for k in range(parts):
        base_loads[k].wait()
        near_loads[k].wait()
        own_loads[k].wait()
        for index in range(k * chunk, (k + 1) * chunk):
            span = slice(index * leaf, (index + 1) * leaf)
            part = leaf_fields[:, index * rank : (index + 1) * rank]
            near[:, span] += own[:, span] + dot(part, bases[index], 1, 1)
        span = pl.ds(k * width, width)
        store = pltpu.make_async_copy(near.at[:, span], out.at[:, span], store_sem.at[k])
        store.start()
        stores.append(store)
    for copy in stores + copies:
        copy.wait()


def rim_kernel(steps, main_hbm, arrived_hbm, out_hbm, main, arrived, load_sem, rim_sem, store_sem):
    count = main.shape[1]
    rim = arrived.shape[2]
    width = count // steps
    spans = [pl.ds(k * width, width) for k in range(steps)]
    loads = [
        pltpu.make_async_copy(main_hbm.at[:, span], main.at[:, span], load_sem.at[k])
        for k, span in enumerate(spans)
    ]
    stores = [
        pltpu.make_async_copy(main.at[:, span], out_hbm.at[:, span], store_sem.at[k])
        for k, span in enumerate(spans)
    ]
    rims = pltpu.make_async_copy(arrived_hbm, arrived, rim_sem)
    rims.start()
    for copy in loads:
        copy.start()
    rims.wait()
    for k in range(steps):
        loads[k].wait()
        if k == 0:
            main[:, :rim] += arrived[0].astype(F32)
        if k == steps - 1:
            main[:, count - rim :] += arrived[1].astype(F32)
        stores[k].start()
    for copy in stores:
        copy.wait()


def on_device(
    points, charges, bases, transfers, parents, couplings, group_couplings, near_pairs, pair_count, far_list
):
    leaves = transfers.shape[1]
    count = points.shape[1]
    leaf = count // leaves
    dim, rhs, rank = points.shape[2], charges.shape[2], bases.shape[2]
    rim = REACH * leaf
    wide = count + 2 * rim
    inner, outer = lax.axis_size("inner"), lax.axis_size("outer")
    pt = jnp.swapaxes(points[0], 0, 1)
    ct = jnp.swapaxes(charges[0], 0, 1)
    pairs = jnp.swapaxes(near_pairs[0], 0, 1)
    leaf_bases = bases[0].reshape(leaves, leaf, rank)
    flat_transfers = transfers[0].reshape(leaves * rank, rank)
    dma = pltpu.SemaphoreType.DMA
    parts = leaves // 8
    halo_points, halo_charges, own, field = pl.pallas_call(
        functools.partial(exchange_kernel, inner, outer, leaves),
        out_shape=[
            jax.ShapeDtypeStruct((2, dim, rim), BF),
            jax.ShapeDtypeStruct((2, rhs, rim), BF),
            jax.ShapeDtypeStruct((rhs, count), F32),
            jax.ShapeDtypeStruct((rhs, rank), BF),
        ],
        in_specs=[ANY] * 7 + [SMEM],
        out_specs=[ANY, ANY, ANY, VMEM],
        scratch_shapes=[
            pltpu.VMEM((dim, count), BF),
            pltpu.VMEM((rhs, count), BF),
            pltpu.VMEM((leaves, leaf, rank), BF),
            pltpu.VMEM((leaves * rank, rank), BF),
            pltpu.VMEM((rank, rank), BF),
            pltpu.VMEM(couplings.shape[1:], BF),
            pltpu.VMEM(group_couplings.shape[1:], BF),
            pltpu.VMEM((rhs, count), F32),
            pltpu.VMEM((rhs, leaves * rank), BF),
            pltpu.VMEM((rhs, rank), F32),
            pltpu.VMEM((inner, rhs, rank), BF),
            pltpu.VMEM((inner, rhs, rank), F32),
            pltpu.VMEM((outer - 1, rhs, rank), F32),
            pltpu.VMEM((2, leaf, leaf), BF),
            dma((6 + parts,)),
            dma((2,)),
            dma((4,)),
            dma((4,)),
            dma((inner,)),
            dma((inner,)),
            dma((outer - 1,)),
            dma((inner,)),
            dma((inner,)),
            dma((outer - 1,)),
        ],
        compiler_params=pltpu.CompilerParams(
            vmem_limit_bytes=LIMIT, collective_id=0, has_side_effects=True
        ),
        name="exchange",
    )(pt, ct, leaf_bases, flat_transfers, parents[0, 0], couplings[0], group_couplings[0], far_list)
    near, halo = pl.pallas_call(
        functools.partial(pair_kernel, leaves, leaf),
        out_shape=[
            jax.ShapeDtypeStruct((rhs, count), F32),
            jax.ShapeDtypeStruct((2, rhs, rim), BF),
        ],
        in_specs=[SMEM, SMEM] + [ANY] * 4,
        out_specs=[ANY, ANY],
        scratch_shapes=[
            pltpu.VMEM((dim, wide), BF),
            pltpu.VMEM((rhs, wide), BF),
            pltpu.VMEM((EXTRA, wide), BF),
            pltpu.VMEM((EXTRA, wide), BF),
            pltpu.VMEM((rhs, wide), F32),
            pltpu.VMEM((2, leaf, leaf), BF),
            pltpu.VMEM((2, leaf, leaf), BF),
            pltpu.VMEM((2, rhs, rim), BF),
            dma((5 + parts,)),
        ],
        compiler_params=pltpu.CompilerParams(vmem_limit_bytes=LIMIT),
        name="pairs",
    )(pairs, pair_count, pt, ct, halo_points, halo_charges)
    main, arrived = pl.pallas_call(
        functools.partial(finish_kernel, inner),
        out_shape=[
            jax.ShapeDtypeStruct((rhs, count), F32),
            jax.ShapeDtypeStruct((2, rhs, rim), BF),
        ],
        in_specs=[ANY] * 6,
        out_specs=[ANY, ANY],
        scratch_shapes=[
            pltpu.VMEM((rhs, count), F32),
            pltpu.VMEM((rhs, count), F32),
            pltpu.VMEM((leaves, leaf, rank), BF),
            pltpu.VMEM((leaves * rank, rank), BF),
            pltpu.VMEM((rhs, rank), BF),
            pltpu.VMEM((rhs, leaves * rank), BF),
            dma((2 + 3 * parts,)),
            dma((parts,)),
            dma((2,)),
            dma((2,)),
        ],
        compiler_params=pltpu.CompilerParams(
            vmem_limit_bytes=LIMIT, collective_id=1, has_side_effects=True
        ),
        name="finish",
    )(halo, near, own, leaf_bases, flat_transfers, field)
    steps = 4
    out = pl.pallas_call(
        functools.partial(rim_kernel, steps),
        out_shape=jax.ShapeDtypeStruct((rhs, count), F32),
        in_specs=[ANY, ANY],
        out_specs=ANY,
        scratch_shapes=[
            pltpu.VMEM((rhs, count), F32),
            pltpu.VMEM((2, rhs, rim), BF),
            dma((steps,)),
            dma,
            dma((steps,)),
        ],
        compiler_params=pltpu.CompilerParams(vmem_limit_bytes=LIMIT),
        name="rims",
    )(main, arrived)
    return jnp.swapaxes(out, 0, 1)[None]


def solution(mesh):
    placed = (
        P("outer", "inner", None),
        P("outer", "inner", None),
        P("outer", "inner", None),
        P("outer", "inner", None, None),
        P("outer", "inner", None, None),
        P("outer", "inner", None, None),
        P("outer", None, None, None),
        P("outer", "inner", None),
        P("outer", "inner"),
        P("outer", "inner"),
    )
    return jax.shard_map(
        on_device, mesh=mesh, in_specs=placed, out_specs=P("outer", "inner", None), check_vma=False
    )
```

```python
import functools

import jax
import jax.numpy as jnp
from jax import lax
from jax.experimental import pallas as pl
from jax.experimental.pallas import tpu as pltpu
from jax.sharding import PartitionSpec as P

REACH = 4
RIDGE = 0.25
EXTRA = 16
GROUP = 4
PAIR_GROUPS = (8, 4, 1)
BF = jnp.bfloat16
F32 = jnp.float32
VMEM = pl.BlockSpec(memory_space=pltpu.VMEM)
SMEM = pl.BlockSpec(memory_space=pltpu.SMEM)
ANY = pl.BlockSpec(memory_space=pl.ANY)
HBM = pl.BlockSpec(memory_space=pltpu.HBM)
MESH = pl.DeviceIdType.MESH


def dot(left, right, left_dim, right_dim):
    return lax.dot_general(
        left, right, (((left_dim,), (right_dim,)), ((), ())), preferred_element_type=F32
    )


def norm_rows(block):
    wide = block.astype(F32)
    total = 0.5 * jnp.sum(wide * wide, 0, keepdims=True)
    high = total.astype(BF).astype(F32)
    rest = total - high
    middle = rest.astype(BF).astype(F32)
    parts = (high, middle, rest - middle)
    row = lax.broadcasted_iota(jnp.int32, (EXTRA, block.shape[1]), 0)
    first = jnp.where((row >= 3) & (row < 6), 1.0, 0.0)
    second = jnp.where(row < 3, 1.0, 0.0)
    for k in range(3):
        first = jnp.where(row == k, -parts[k], first)
        second = jnp.where(row == 3 + k, -parts[k], second)
    return first.astype(BF), second.astype(BF)


def columns(index, width):
    return pl.ds(pl.multiple_of(index * width, width), width)


def tile_of(points, firsts, seconds, cols_a, cols_b):
    left = jnp.concatenate([points[:, cols_a], firsts[:, cols_a]], 0)
    right = jnp.concatenate([points[:, cols_b], seconds[:, cols_b]], 0)
    return jnp.exp(dot(left, right, 0, 0)).astype(BF)


def exchange_kernel(
    inner, outer, leaves,
    pt_hbm, ct_hbm, bases_hbm, transfers_hbm, parent_hbm, couplings_hbm, group_couplings_hbm, far,
    halo_points, halo_charges, near_hbm, field_out,
    points, charges, bases, transfers, parent, couplings, group_couplings, near,
    skeletons, term, slots, gathered, parts, tiles,
    load_sem, near_sem, halo_send, halo_recv, node_send, node_recv, term_send, term_recv,
    field_send, field_recv,
):
    me, group = lax.axis_index("inner"), lax.axis_index("outer")
    right, left = lax.rem(me + 1, inner), lax.rem(me + inner - 1, inner)
    rhs, count = ct_hbm.shape
    leaf = count // leaves
    rim = REACH * leaf
    rank = parent.shape[1]
    chunk = 8
    half = inner // 2
    roots = [
        (k, h, h * half + k * (half // (outer - 1))) for k in range(outer - 1) for h in range(2)
    ]
    peers = [lax.rem(me + k, inner) for k in range(1, inner)]
    sources = [lax.rem(group + k, outer) for k in range(1, outer)]
    sinks = [lax.rem(group + outer - k, outer) for k in range(1, outer)]
    loads = [
        pltpu.make_async_copy(ct_hbm, charges, load_sem.at[0]),
        pltpu.make_async_copy(transfers_hbm, transfers, load_sem.at[1]),
        pltpu.make_async_copy(pt_hbm, points, load_sem.at[2]),
        pltpu.make_async_copy(parent_hbm, parent, load_sem.at[3]),
        pltpu.make_async_copy(couplings_hbm, couplings, load_sem.at[4]),
        pltpu.make_async_copy(group_couplings_hbm, group_couplings, load_sem.at[5]),
    ]
    base_loads = [
        pltpu.make_async_copy(
            bases_hbm.at[pl.ds(k * chunk, chunk)], bases.at[pl.ds(k * chunk, chunk)], load_sem.at[6 + k]
        )
        for k in range(leaves // chunk)
    ]
    loads[0].start()
    for copy in base_loads:
        copy.start()
    loads[1].start()
    loads[3].start()
    barrier = pltpu.get_barrier_semaphore()
    for k, _, root in roots:

        @pl.when(me == root)
        def _(source=sources[k]):
            def greet(index, carry):
                pl.semaphore_signal(
                    barrier, inc=1, device_id={"inner": index, "outer": source}, device_id_type=MESH
                )
                return carry

            lax.fori_loop(0, inner, greet, 0)

    for peer in peers:
        pl.semaphore_signal(barrier, inc=1, device_id={"inner": peer}, device_id_type=MESH)

    loads[0].wait()
    for k, copy in enumerate(base_loads):
        copy.wait()
        for index in range(k * chunk, (k + 1) * chunk):
            block = charges[:, index * leaf : (index + 1) * leaf]
            skeletons[:, index * rank : (index + 1) * rank] = dot(block, bases[index], 1, 0).astype(BF)
    for k in (2, 4, 5):
        loads[k].start()
    loads[1].wait()
    node = dot(skeletons[...], transfers[...], 1, 0).astype(BF)
    slots[me] = node
    loads[3].wait()
    term[...] = dot(node, parent[...], 1, 0)
    pl.semaphore_wait(barrier, inner - 1 + len(roots))

    def remote(source, target, send, recv, **where):
        return pltpu.make_async_remote_copy(
            src_ref=source, dst_ref=target, send_sem=send, recv_sem=recv,
            device_id=where, device_id_type=MESH,
        )

    term_copies = [
        remote(term, gathered.at[me], term_send.at[at], term_recv.at[me], inner=root, outer=sinks[k])
        for at, (k, _, root) in enumerate(roots)
    ]
    for copy in term_copies:
        copy.start()
    halo_copies = [
        remote(
            source.at[:, pl.ds(begin, rim)], target, halo_send.at[k], halo_recv.at[k], inner=peer
        )
        for k, (source, target, peer, begin) in enumerate((
            (pt_hbm, halo_points.at[0], right, count - rim),
            (pt_hbm, halo_points.at[1], left, 0),
            (ct_hbm, halo_charges.at[0], right, count - rim),
            (ct_hbm, halo_charges.at[1], left, 0),
        ))
    ]
    node_copies = [
        remote(slots.at[me], slots.at[me], node_send.at[k], node_recv.at[me], inner=peer)
        for k, peer in enumerate(peers)
    ]
    field_copies = [
        [
            remote(parts.at[k], parts.at[k], field_send.at[peer], field_recv.at[k], inner=peer)
            for peer in range(h * half, (h + 1) * half)
            if peer != root
        ]
        for k, h, root in roots
    ]
    for copy in halo_copies + node_copies:
        copy.start()
    loads[2].wait()
    edge = leaf // 2

    def own_tile(index, slot):
        block = points[:, columns(index, leaf)]
        first, second = norm_rows(block)
        left_form = jnp.concatenate([block, first], 0)
        right_form = jnp.concatenate([block, second], 0)
        upper = jnp.exp(dot(left_form[:, :edge], right_form, 0, 0)).astype(BF)
        tiles[slot, :edge] = upper
        tiles[slot, edge:, :edge] = upper[:, edge:].T
        tiles[slot, edge:, edge:] = jnp.exp(
            dot(left_form[:, edge:], right_form[:, edge:], 0, 0)
        ).astype(BF)

    def diagonal(index, carry):
        for k in range(GROUP):
            at = index * GROUP + k
            own_tile(jnp.minimum(at + 1, leaves - 1), (k + 1) % 2)
            cols = columns(at, leaf)
            own = charges[:, cols]
            near[:, cols] = RIDGE * own.astype(F32) + dot(own, tiles[k % 2], 1, 0)
        return carry

    own_tile(0, 0)
    total = leaves // GROUP
    stop = 3 * total // 8
    lax.fori_loop(0, stop, diagonal, 0)
    spans = [pl.ds(0, stop * GROUP * leaf), pl.ds(stop * GROUP * leaf, (total - stop) * GROUP * leaf)]
    near_copies = [
        pltpu.make_async_copy(near.at[:, span], near_hbm.at[:, span], near_sem.at[k])
        for k, span in enumerate(spans)
    ]
    near_copies[0].start()
    loads[4].wait()
    loads[5].wait()
    for at, (k, _, root) in enumerate(roots):

        @pl.when(me == root)
        def _(at=at, k=k):
            def arrive(index, carry):
                pltpu.make_async_copy(term, gathered.at[index], term_recv.at[index]).wait()
                return carry

            lax.fori_loop(0, inner, arrive, 0)
            skeleton = jnp.sum(gathered[...], 0).astype(BF)
            parts[k] = dot(skeleton, group_couplings[sources[k]], 1, 1)
            for copy in field_copies[at]:
                copy.start()

    lax.fori_loop(stop, total, diagonal, 0)
    near_copies[1].start()
    for peer in peers:
        pltpu.make_async_copy(slots.at[me], slots.at[peer], node_recv.at[peer]).wait()
    field = jnp.zeros((rhs, rank), F32)
    for j in range(couplings.shape[0]):
        field += dot(slots[far[0, j]], couplings[j], 1, 1)
    for k in range(outer - 1):
        first_root, second_root = [root for at, _, root in roots if at == k]

        @pl.when((me != first_root) & (me != second_root))
        def _(k=k):
            pltpu.make_async_copy(parts.at[k], parts.at[k], field_recv.at[k]).wait()

    group_field = jnp.sum(parts[...], 0).astype(BF)
    field_out[...] = (field + dot(group_field, parent[...], 1, 1)).astype(BF)
    for copy in term_copies + node_copies:
        copy.wait_send()
    for at, (_, _, root) in enumerate(roots):

        @pl.when(me == root)
        def _(at=at):
            for copy in field_copies[at]:
                copy.wait_send()

    for copy in near_copies:
        copy.wait()
    for copy in halo_copies:
        copy.wait()


def pair_kernel(
    leaves, leaf,
    pairs, live, pt_hbm, ct_hbm, halo_points, halo_charges,
    out_near, out_halo,
    points, charges, firsts, seconds, totals, tiles, flipped, halo, sem,
):
    rim = REACH * leaf
    count = leaves * leaf
    chunk = 8
    spots = (pl.ds(0, rim), pl.ds(rim + count, rim))
    own = pl.ds(rim, count)
    copies = [
        pltpu.make_async_copy(halo_points.at[0], points.at[:, spots[0]], sem.at[0]),
        pltpu.make_async_copy(halo_points.at[1], points.at[:, spots[1]], sem.at[1]),
    ]
    copies += [
        pltpu.make_async_copy(
            pt_hbm.at[:, pl.ds(k * chunk * leaf, chunk * leaf)],
            points.at[:, pl.ds(rim + k * chunk * leaf, chunk * leaf)],
            sem.at[2 + k],
        )
        for k in range(leaves // chunk)
    ]
    at = len(copies)
    charge_copies = [
        pltpu.make_async_copy(ct_hbm, charges.at[:, own], sem.at[at]),
        pltpu.make_async_copy(halo_charges.at[0], charges.at[:, spots[0]], sem.at[at + 1]),
        pltpu.make_async_copy(halo_charges.at[1], charges.at[:, spots[1]], sem.at[at + 2]),
    ]
    for copy in copies + charge_copies:
        copy.start()
    totals[...] = jnp.zeros_like(totals)

    def build(index, carry):
        cols = columns(index, leaf)
        firsts[:, cols], seconds[:, cols] = norm_rows(points[:, cols])
        return carry

    spans_built = [(0, REACH), (REACH + leaves, 2 * REACH + leaves)]
    spans_built += [(REACH + k * chunk, REACH + (k + 1) * chunk) for k in range(leaves // chunk)]
    for copy, (low, high) in zip(copies, spans_built):
        copy.wait()
        lax.fori_loop(low, high, build, 0, unroll=2)
    for copy in charge_copies:
        copy.wait()
    number = live[0, 0]

    def spans(index):
        return columns(pairs[0, index] + REACH, leaf), columns(pairs[1, index], leaf)

    def make(index, slot):
        cols_a, cols_b = spans(jnp.minimum(index, number - 1))
        tile = tile_of(points, firsts, seconds, cols_a, cols_b)
        tiles[slot] = tile
        flipped[slot] = tile.T

    def use(index, slot):
        cols_a, cols_b = spans(index)
        totals[:, cols_b] += dot(charges[:, cols_a], tiles[slot], 1, 0)
        totals[:, cols_a] += dot(charges[:, cols_b], flipped[slot], 1, 0)

    make(0, 0)
    done = 0
    for size in PAIR_GROUPS:

        def block(index, carry, size=size, done=done):
            for k in range(size):
                at = done + index * size + k
                slot = k % 2 if size > 1 else lax.rem(at, 2)
                make(at + 1, 1 - slot)
                use(at, slot)
            return carry

        blocks = (number - done) // size
        lax.fori_loop(0, blocks, block, 0)
        done += blocks * size
    write = pltpu.make_async_copy(totals.at[:, own], out_near, sem.at[0])
    write.start()
    for k, spot in enumerate(spots):
        halo[k] = totals[:, spot].astype(BF)
    halo_write = pltpu.make_async_copy(halo, out_halo, sem.at[1])
    halo_write.start()
    halo_write.wait()
    write.wait()


def finish_kernel(
    inner,
    halo, near_hbm, own_hbm, bases_hbm, transfers_hbm, field_hbm,
    out, arrived,
    near, own, bases, transfers, field, leaf_fields, load_sem, store_sem, send_sem, recv_sem,
):
    me = lax.axis_index("inner")
    right, left = lax.rem(me + 1, inner), lax.rem(me + inner - 1, inner)
    leaves, leaf, rank = bases.shape
    chunk = 8
    parts = leaves // chunk
    width = chunk * leaf
    barrier = pltpu.get_barrier_semaphore()
    for peer in (left, right):
        pl.semaphore_signal(barrier, inc=1, device_id={"inner": peer}, device_id_type=MESH)
    loads = [
        pltpu.make_async_copy(transfers_hbm, transfers, load_sem.at[0]),
        pltpu.make_async_copy(field_hbm, field, load_sem.at[1 + 3 * (leaves // chunk)]),
    ]
    near_loads, own_loads, base_loads = [], [], []
    for k in range(parts):
        span = pl.ds(k * width, width)
        leaf_span = pl.ds(k * chunk, chunk)
        base_loads.append(
            pltpu.make_async_copy(bases_hbm.at[leaf_span], bases.at[leaf_span], load_sem.at[1 + k])
        )
        near_loads.append(
            pltpu.make_async_copy(near_hbm.at[:, span], near.at[:, span], load_sem.at[1 + parts + k])
        )
        own_loads.append(
            pltpu.make_async_copy(own_hbm.at[:, span], own.at[:, span], load_sem.at[1 + 2 * parts + k])
        )
    for copy in loads:
        copy.start()
    for group in zip(base_loads, near_loads, own_loads):
        for copy in group:
            copy.start()
    pl.semaphore_wait(barrier, 2)
    copies = []
    for k, peer in enumerate((left, right)):
        copy = pltpu.make_async_remote_copy(
            src_ref=halo.at[k], dst_ref=arrived.at[1 - k], send_sem=send_sem.at[k],
            recv_sem=recv_sem.at[1 - k], device_id={"inner": peer}, device_id_type=MESH,
        )
        copy.start()
        copies.append(copy)
    for copy in loads:
        copy.wait()
    leaf_fields[...] = dot(field[...], transfers[...], 1, 1).astype(BF)
    stores = []
    for k in range(parts):
        base_loads[k].wait()
        near_loads[k].wait()
        own_loads[k].wait()
        for index in range(k * chunk, (k + 1) * chunk):
            span = slice(index * leaf, (index + 1) * leaf)
            part = leaf_fields[:, index * rank : (index + 1) * rank]
            near[:, span] += own[:, span] + dot(part, bases[index], 1, 1)
        span = pl.ds(k * width, width)
        store = pltpu.make_async_copy(near.at[:, span], out.at[:, span], store_sem.at[k])
        store.start()
        stores.append(store)
    for copy in stores + copies:
        copy.wait()


def rim_kernel(steps, main_hbm, arrived_hbm, out_hbm, main, arrived, load_sem, rim_sem, store_sem):
    count = main.shape[1]
    rim = arrived.shape[2]
    width = count // steps
    spans = [pl.ds(k * width, width) for k in range(steps)]
    loads = [
        pltpu.make_async_copy(main_hbm.at[:, span], main.at[:, span], load_sem.at[k])
        for k, span in enumerate(spans)
    ]
    stores = [
        pltpu.make_async_copy(main.at[:, span], out_hbm.at[:, span], store_sem.at[k])
        for k, span in enumerate(spans)
    ]
    rims = pltpu.make_async_copy(arrived_hbm, arrived, rim_sem)
    rims.start()
    for copy in loads:
        copy.start()
    rims.wait()
    for k in range(steps):
        loads[k].wait()
        if k == 0:
            main[:, :rim] += arrived[0].astype(F32)
        if k == steps - 1:
            main[:, count - rim :] += arrived[1].astype(F32)
        stores[k].start()
    for copy in stores:
        copy.wait()


def on_device(
    points, charges, bases, transfers, parents, couplings, group_couplings, near_pairs, pair_count, far_list
):
    leaves = transfers.shape[1]
    count = points.shape[1]
    leaf = count // leaves
    dim, rhs, rank = points.shape[2], charges.shape[2], bases.shape[2]
    rim = REACH * leaf
    wide = count + 2 * rim
    inner, outer = lax.axis_size("inner"), lax.axis_size("outer")
    pt = jnp.swapaxes(points[0], 0, 1)
    ct = jnp.swapaxes(charges[0], 0, 1)
    pairs = jnp.swapaxes(near_pairs[0], 0, 1)
    leaf_bases = bases[0].reshape(leaves, leaf, rank)
    flat_transfers = transfers[0].reshape(leaves * rank, rank)
    dma = pltpu.SemaphoreType.DMA
    parts = leaves // 8
    halo_points, halo_charges, own, field = pl.pallas_call(
        functools.partial(exchange_kernel, inner, outer, leaves),
        out_shape=[
            jax.ShapeDtypeStruct((2, dim, rim), BF),
            jax.ShapeDtypeStruct((2, rhs, rim), BF),
            jax.ShapeDtypeStruct((rhs, count), F32),
            jax.ShapeDtypeStruct((rhs, rank), BF),
        ],
        in_specs=[HBM] * 7 + [SMEM],
        out_specs=[ANY, ANY, ANY, VMEM],
        scratch_shapes=[
            pltpu.VMEM((dim, count), BF),
            pltpu.VMEM((rhs, count), BF),
            pltpu.VMEM((leaves, leaf, rank), BF),
            pltpu.VMEM((leaves * rank, rank), BF),
            pltpu.VMEM((rank, rank), BF),
            pltpu.VMEM(couplings.shape[1:], BF),
            pltpu.VMEM(group_couplings.shape[1:], BF),
            pltpu.VMEM((rhs, count), F32),
            pltpu.VMEM((rhs, leaves * rank), BF),
            pltpu.VMEM((rhs, rank), F32),
            pltpu.VMEM((inner, rhs, rank), BF),
            pltpu.VMEM((inner, rhs, rank), F32),
            pltpu.VMEM((outer - 1, rhs, rank), F32),
            pltpu.VMEM((2, leaf, leaf), BF),
            dma((6 + parts,)),
            dma((2,)),
            dma((4,)),
            dma((4,)),
            dma((inner,)),
            dma((inner,)),
            dma((2 * (outer - 1),)),
            dma((inner,)),
            dma((inner,)),
            dma((outer - 1,)),
        ],
        compiler_params=pltpu.CompilerParams(
            vmem_limit_bytes=56 * 2**20, collective_id=0, has_side_effects=True
        ),
        name="exchange",
    )(pt, ct, leaf_bases, flat_transfers, parents[0, 0], couplings[0], group_couplings[0], far_list)
    near, halo = pl.pallas_call(
        functools.partial(pair_kernel, leaves, leaf),
        out_shape=[
            jax.ShapeDtypeStruct((rhs, count), F32),
            jax.ShapeDtypeStruct((2, rhs, rim), BF),
        ],
        in_specs=[SMEM, SMEM] + [ANY] * 4,
        out_specs=[ANY, ANY],
        scratch_shapes=[
            pltpu.VMEM((dim, wide), BF),
            pltpu.VMEM((rhs, wide), BF),
            pltpu.VMEM((EXTRA, wide), BF),
            pltpu.VMEM((EXTRA, wide), BF),
            pltpu.VMEM((rhs, wide), F32),
            pltpu.VMEM((2, leaf, leaf), BF),
            pltpu.VMEM((2, leaf, leaf), BF),
            pltpu.VMEM((2, rhs, rim), BF),
            dma((5 + parts,)),
        ],
        compiler_params=pltpu.CompilerParams(vmem_limit_bytes=56 * 2**20),
        name="pairs",
    )(pairs, pair_count, pt, ct, halo_points, halo_charges)
    main, arrived = pl.pallas_call(
        functools.partial(finish_kernel, inner),
        out_shape=[
            jax.ShapeDtypeStruct((rhs, count), F32),
            jax.ShapeDtypeStruct((2, rhs, rim), BF),
        ],
        in_specs=[ANY] * 3 + [HBM, HBM, ANY],
        out_specs=[ANY, ANY],
        scratch_shapes=[
            pltpu.VMEM((rhs, count), F32),
            pltpu.VMEM((rhs, count), F32),
            pltpu.VMEM((leaves, leaf, rank), BF),
            pltpu.VMEM((leaves * rank, rank), BF),
            pltpu.VMEM((rhs, rank), BF),
            pltpu.VMEM((rhs, leaves * rank), BF),
            dma((2 + 3 * parts,)),
            dma((parts,)),
            dma((2,)),
            dma((2,)),
        ],
        compiler_params=pltpu.CompilerParams(
            vmem_limit_bytes=56 * 2**20, collective_id=1, has_side_effects=True
        ),
        name="finish",
    )(halo, near, own, leaf_bases, flat_transfers, field)
    steps = 4
    out = pl.pallas_call(
        functools.partial(rim_kernel, steps),
        out_shape=jax.ShapeDtypeStruct((rhs, count), F32),
        in_specs=[ANY, ANY],
        out_specs=HBM,
        scratch_shapes=[
            pltpu.VMEM((rhs, count), F32),
            pltpu.VMEM((2, rhs, rim), BF),
            dma((steps,)),
            dma,
            dma((steps,)),
        ],
        compiler_params=pltpu.CompilerParams(vmem_limit_bytes=56 * 2**20),
        name="rims",
    )(main, arrived)
    return jnp.swapaxes(out, 0, 1)[None]


def solution(mesh):
    placed = (
        P("outer", "inner", None),
        P("outer", "inner", None),
        P("outer", "inner", None),
        P("outer", "inner", None, None),
        P("outer", "inner", None, None),
        P("outer", "inner", None, None),
        P("outer", None, None, None),
        P("outer", "inner", None),
        P("outer", "inner"),
        P("outer", "inner"),
    )
    return jax.shard_map(
        on_device, mesh=mesh, in_specs=placed, out_specs=P("outer", "inner", None), check_vma=False
    )
```

```python
import functools

import jax
import jax.numpy as jnp
from jax import lax
from jax.experimental import pallas as pl
from jax.experimental.pallas import tpu as pltpu
from jax.sharding import PartitionSpec as P

REACH = 4
RIDGE = 0.25
EXTRA = 16
GROUP = 4
PAIR_GROUPS = (8, 4)
BF = jnp.bfloat16
F32 = jnp.float32
VMEM = pl.BlockSpec(memory_space=pltpu.VMEM)
SMEM = pl.BlockSpec(memory_space=pltpu.SMEM)
ANY = pl.BlockSpec(memory_space=pl.ANY)
HBM = pl.BlockSpec(memory_space=pltpu.HBM)
MESH = pl.DeviceIdType.MESH


def dot(left, right, left_dim, right_dim):
    return lax.dot_general(
        left, right, (((left_dim,), (right_dim,)), ((), ())), preferred_element_type=F32
    )


def norm_rows(block):
    wide = block.astype(F32)
    total = 0.5 * jnp.sum(wide * wide, 0, keepdims=True)
    high = total.astype(BF).astype(F32)
    rest = total - high
    middle = rest.astype(BF).astype(F32)
    parts = (high, middle, rest - middle)
    row = lax.broadcasted_iota(jnp.int32, (EXTRA, block.shape[1]), 0)
    first = jnp.where((row >= 3) & (row < 6), 1.0, 0.0)
    second = jnp.where(row < 3, 1.0, 0.0)
    for k in range(3):
        first = jnp.where(row == k, -parts[k], first)
        second = jnp.where(row == 3 + k, -parts[k], second)
    return first.astype(BF), second.astype(BF)


def columns(index, width):
    return pl.ds(pl.multiple_of(index * width, width), width)


def tile_of(points, firsts, seconds, cols_a, cols_b):
    left = jnp.concatenate([points[:, cols_a], firsts[:, cols_a]], 0)
    right = jnp.concatenate([points[:, cols_b], seconds[:, cols_b]], 0)
    return jnp.exp(dot(left, right, 0, 0)).astype(BF)


def exchange_kernel(
    inner, outer, leaves,
    pt_hbm, ct_hbm, bases_hbm, transfers_hbm, parent_hbm, couplings_hbm, group_couplings_hbm, far,
    halo_points, halo_charges, near_hbm, field_out,
    points, charges, bases, transfers, parent, couplings, group_couplings, near,
    skeletons, term, slots, gathered, parts, tiles,
    load_sem, near_sem, halo_send, halo_recv, node_send, node_recv, term_send, term_recv,
    field_send, field_recv,
):
    me, group = lax.axis_index("inner"), lax.axis_index("outer")
    right, left = lax.rem(me + 1, inner), lax.rem(me + inner - 1, inner)
    rhs, count = ct_hbm.shape
    leaf = count // leaves
    rim = REACH * leaf
    rank = parent.shape[1]
    chunk = 8
    half = inner // 2
    roots = [
        (k, h, h * half + k * (half // (outer - 1))) for k in range(outer - 1) for h in range(2)
    ]
    peers = [lax.rem(me + k, inner) for k in range(1, inner)]
    sources = [lax.rem(group + k, outer) for k in range(1, outer)]
    sinks = [lax.rem(group + outer - k, outer) for k in range(1, outer)]
    loads = [
        pltpu.make_async_copy(ct_hbm, charges, load_sem.at[0]),
        pltpu.make_async_copy(transfers_hbm, transfers, load_sem.at[1]),
        pltpu.make_async_copy(pt_hbm, points, load_sem.at[2]),
        pltpu.make_async_copy(parent_hbm, parent, load_sem.at[3]),
        pltpu.make_async_copy(couplings_hbm, couplings, load_sem.at[4]),
        pltpu.make_async_copy(group_couplings_hbm, group_couplings, load_sem.at[5]),
    ]
    base_loads = [
        pltpu.make_async_copy(
            bases_hbm.at[pl.ds(k * chunk, chunk)], bases.at[pl.ds(k * chunk, chunk)], load_sem.at[6 + k]
        )
        for k in range(leaves // chunk)
    ]
    loads[0].start()
    for copy in base_loads:
        copy.start()
    loads[1].start()
    loads[3].start()
    barrier = pltpu.get_barrier_semaphore()
    for k, _, root in roots:

        @pl.when(me == root)
        def _(source=sources[k]):
            def greet(index, carry):
                pl.semaphore_signal(
                    barrier, inc=1, device_id={"inner": index, "outer": source}, device_id_type=MESH
                )
                return carry

            lax.fori_loop(0, inner, greet, 0)

    for peer in peers:
        pl.semaphore_signal(barrier, inc=1, device_id={"inner": peer}, device_id_type=MESH)

    loads[0].wait()
    for k, copy in enumerate(base_loads):
        copy.wait()
        for index in range(k * chunk, (k + 1) * chunk):
            block = charges[:, index * leaf : (index + 1) * leaf]
            skeletons[:, index * rank : (index + 1) * rank] = dot(block, bases[index], 1, 0).astype(BF)
    for k in (2, 4, 5):
        loads[k].start()
    loads[1].wait()
    node = dot(skeletons[...], transfers[...], 1, 0).astype(BF)
    slots[me] = node
    loads[3].wait()
    term[...] = dot(node, parent[...], 1, 0)
    pl.semaphore_wait(barrier, inner - 1 + len(roots))

    def remote(source, target, send, recv, **where):
        return pltpu.make_async_remote_copy(
            src_ref=source, dst_ref=target, send_sem=send, recv_sem=recv,
            device_id=where, device_id_type=MESH,
        )

    term_copies = [
        remote(term, gathered.at[me], term_send.at[at], term_recv.at[me], inner=root, outer=sinks[k])
        for at, (k, _, root) in enumerate(roots)
    ]
    for copy in term_copies:
        copy.start()
    halo_copies = [
        remote(
            source.at[:, pl.ds(begin, rim)], target, halo_send.at[k], halo_recv.at[k], inner=peer
        )
        for k, (source, target, peer, begin) in enumerate((
            (pt_hbm, halo_points.at[0], right, count - rim),
            (pt_hbm, halo_points.at[1], left, 0),
            (ct_hbm, halo_charges.at[0], right, count - rim),
            (ct_hbm, halo_charges.at[1], left, 0),
        ))
    ]
    node_copies = [
        remote(slots.at[me], slots.at[me], node_send.at[k], node_recv.at[me], inner=peer)
        for k, peer in enumerate(peers)
    ]
    field_copies = [
        [
            remote(parts.at[k], parts.at[k], field_send.at[peer], field_recv.at[k], inner=peer)
            for peer in range(h * half, (h + 1) * half)
            if peer != root
        ]
        for k, h, root in roots
    ]
    for copy in halo_copies + node_copies:
        copy.start()
    loads[2].wait()
    edge = leaf // 2

    def own_tile(index, slot):
        block = points[:, columns(index, leaf)]
        first, second = norm_rows(block)
        left_form = jnp.concatenate([block, first], 0)
        right_form = jnp.concatenate([block, second], 0)
        upper = jnp.exp(dot(left_form[:, :edge], right_form, 0, 0)).astype(BF)
        tiles[slot, :edge] = upper
        tiles[slot, edge:, :edge] = upper[:, edge:].T
        tiles[slot, edge:, edge:] = jnp.exp(
            dot(left_form[:, edge:], right_form[:, edge:], 0, 0)
        ).astype(BF)

    def diagonal(index, carry):
        for k in range(GROUP):
            at = index * GROUP + k
            own_tile(jnp.minimum(at + 1, leaves - 1), (k + 1) % 2)
            cols = columns(at, leaf)
            own = charges[:, cols]
            near[:, cols] = RIDGE * own.astype(F32) + dot(own, tiles[k % 2], 1, 0)
        return carry

    own_tile(0, 0)
    total = leaves // GROUP
    stop = 3 * total // 8
    lax.fori_loop(0, stop, diagonal, 0)
    spans = [pl.ds(0, stop * GROUP * leaf), pl.ds(stop * GROUP * leaf, (total - stop) * GROUP * leaf)]
    near_copies = [
        pltpu.make_async_copy(near.at[:, span], near_hbm.at[:, span], near_sem.at[k])
        for k, span in enumerate(spans)
    ]
    near_copies[0].start()
    loads[4].wait()
    loads[5].wait()
    for at, (k, _, root) in enumerate(roots):

        @pl.when(me == root)
        def _(at=at, k=k):
            def arrive(index, carry):
                pltpu.make_async_copy(term, gathered.at[index], term_recv.at[index]).wait()
                return carry

            lax.fori_loop(0, inner, arrive, 0)
            skeleton = jnp.sum(gathered[...], 0).astype(BF)
            parts[k] = dot(skeleton, group_couplings[sources[k]], 1, 1)
            for copy in field_copies[at]:
                copy.start()

    lax.fori_loop(stop, total, diagonal, 0)
    near_copies[1].start()
    for peer in peers:
        pltpu.make_async_copy(slots.at[me], slots.at[peer], node_recv.at[peer]).wait()
    field = jnp.zeros((rhs, rank), F32)
    for j in range(couplings.shape[0]):
        field += dot(slots[far[0, j]], couplings[j], 1, 1)
    for k in range(outer - 1):
        first_root, second_root = [root for at, _, root in roots if at == k]

        @pl.when((me != first_root) & (me != second_root))
        def _(k=k):
            pltpu.make_async_copy(parts.at[k], parts.at[k], field_recv.at[k]).wait()

    group_field = jnp.sum(parts[...], 0).astype(BF)
    field_out[...] = (field + dot(group_field, parent[...], 1, 1)).astype(BF)
    for copy in term_copies + node_copies:
        copy.wait_send()
    for at, (_, _, root) in enumerate(roots):

        @pl.when(me == root)
        def _(at=at):
            for copy in field_copies[at]:
                copy.wait_send()

    for copy in near_copies:
        copy.wait()
    for copy in halo_copies:
        copy.wait()


def pair_kernel(
    leaves, leaf,
    pairs, live, pt_hbm, ct_hbm, halo_points, halo_charges,
    out_near, out_halo,
    points, charges, firsts, seconds, totals, tiles, flipped, halo, sem,
):
    rim = REACH * leaf
    count = leaves * leaf
    chunk = 8
    spots = (pl.ds(0, rim), pl.ds(rim + count, rim))
    own = pl.ds(rim, count)
    copies = [
        pltpu.make_async_copy(halo_points.at[0], points.at[:, spots[0]], sem.at[0]),
        pltpu.make_async_copy(halo_points.at[1], points.at[:, spots[1]], sem.at[1]),
    ]
    copies += [
        pltpu.make_async_copy(
            pt_hbm.at[:, pl.ds(k * chunk * leaf, chunk * leaf)],
            points.at[:, pl.ds(rim + k * chunk * leaf, chunk * leaf)],
            sem.at[2 + k],
        )
        for k in range(leaves // chunk)
    ]
    at = len(copies)
    charge_copies = [
        pltpu.make_async_copy(ct_hbm, charges.at[:, own], sem.at[at]),
        pltpu.make_async_copy(halo_charges.at[0], charges.at[:, spots[0]], sem.at[at + 1]),
        pltpu.make_async_copy(halo_charges.at[1], charges.at[:, spots[1]], sem.at[at + 2]),
    ]
    for copy in copies + charge_copies:
        copy.start()
    totals[...] = jnp.zeros_like(totals)

    def build(index, carry):
        cols = columns(index, leaf)
        firsts[:, cols], seconds[:, cols] = norm_rows(points[:, cols])
        return carry

    spans_built = [(0, REACH), (REACH + leaves, 2 * REACH + leaves)]
    spans_built += [(REACH + k * chunk, REACH + (k + 1) * chunk) for k in range(leaves // chunk)]
    for copy, (low, high) in zip(copies, spans_built):
        copy.wait()
        lax.fori_loop(low, high, build, 0, unroll=2)
    for copy in charge_copies:
        copy.wait()
    number = live[0, 0]

    spare = leaves + 2 * REACH

    def ends(index):
        at = jnp.minimum(index, number - 1)
        return pairs[0, at] + REACH, pairs[1, at]

    def make(index, slot):
        a, b = ends(index)
        tile = tile_of(points, firsts, seconds, columns(a, leaf), columns(b, leaf))
        tiles[slot] = tile
        flipped[slot] = tile.T

    def use(index, slot):
        a, b = ends(index)
        to_a = columns(jnp.where(index < number, a, spare), leaf)
        to_b = columns(jnp.where(index < number, b, spare), leaf)
        totals[:, to_b] += dot(charges[:, columns(a, leaf)], tiles[slot], 1, 0)
        totals[:, to_a] += dot(charges[:, columns(b, leaf)], flipped[slot], 1, 0)

    make(0, 0)
    done = 0
    for size in PAIR_GROUPS:

        def block(index, carry, size=size, done=done):
            for k in range(size):
                at = done + index * size + k
                make(at + 1, (k + 1) % 2)
                use(at, k % 2)
            return carry

        left = number - done
        blocks = (left + size - 1) // size if size == PAIR_GROUPS[-1] else left // size
        lax.fori_loop(0, blocks, block, 0)
        done += blocks * size
    write = pltpu.make_async_copy(totals.at[:, own], out_near, sem.at[0])
    write.start()
    for k, spot in enumerate(spots):
        halo[k] = totals[:, spot].astype(BF)
    halo_write = pltpu.make_async_copy(halo, out_halo, sem.at[1])
    halo_write.start()
    halo_write.wait()
    write.wait()


def finish_kernel(
    inner,
    halo, near_hbm, own_hbm, bases_hbm, transfers_hbm, field_hbm,
    out, arrived,
    near, own, bases, transfers, field, leaf_fields, load_sem, store_sem, send_sem, recv_sem,
):
    me = lax.axis_index("inner")
    right, left = lax.rem(me + 1, inner), lax.rem(me + inner - 1, inner)
    leaves, leaf, rank = bases.shape
    chunk = 8
    parts = leaves // chunk
    width = chunk * leaf
    barrier = pltpu.get_barrier_semaphore()
    for peer in (left, right):
        pl.semaphore_signal(barrier, inc=1, device_id={"inner": peer}, device_id_type=MESH)
    loads = [
        pltpu.make_async_copy(transfers_hbm, transfers, load_sem.at[0]),
        pltpu.make_async_copy(field_hbm, field, load_sem.at[1 + 3 * (leaves // chunk)]),
    ]
    near_loads, own_loads, base_loads = [], [], []
    for k in range(parts):
        span = pl.ds(k * width, width)
        leaf_span = pl.ds(k * chunk, chunk)
        base_loads.append(
            pltpu.make_async_copy(bases_hbm.at[leaf_span], bases.at[leaf_span], load_sem.at[1 + k])
        )
        near_loads.append(
            pltpu.make_async_copy(near_hbm.at[:, span], near.at[:, span], load_sem.at[1 + parts + k])
        )
        own_loads.append(
            pltpu.make_async_copy(own_hbm.at[:, span], own.at[:, span], load_sem.at[1 + 2 * parts + k])
        )
    for copy in loads:
        copy.start()
    for group in zip(base_loads, near_loads, own_loads):
        for copy in group:
            copy.start()
    pl.semaphore_wait(barrier, 2)
    copies = []
    for k, peer in enumerate((left, right)):
        copy = pltpu.make_async_remote_copy(
            src_ref=halo.at[k], dst_ref=arrived.at[1 - k], send_sem=send_sem.at[k],
            recv_sem=recv_sem.at[1 - k], device_id={"inner": peer}, device_id_type=MESH,
        )
        copy.start()
        copies.append(copy)
    for copy in loads:
        copy.wait()
    leaf_fields[...] = dot(field[...], transfers[...], 1, 1).astype(BF)
    stores = []
    for k in range(parts):
        base_loads[k].wait()
        near_loads[k].wait()
        own_loads[k].wait()
        for index in range(k * chunk, (k + 1) * chunk):
            span = slice(index * leaf, (index + 1) * leaf)
            part = leaf_fields[:, index * rank : (index + 1) * rank]
            near[:, span] += own[:, span] + dot(part, bases[index], 1, 1)
        span = pl.ds(k * width, width)
        store = pltpu.make_async_copy(near.at[:, span], out.at[:, span], store_sem.at[k])
        store.start()
        stores.append(store)
    for copy in stores + copies:
        copy.wait()


def rim_kernel(steps, main_hbm, arrived_hbm, out_hbm, main, arrived, load_sem, rim_sem, store_sem):
    count = main.shape[1]
    rim = arrived.shape[2]
    width = count // steps
    spans = [pl.ds(k * width, width) for k in range(steps)]
    loads = [
        pltpu.make_async_copy(main_hbm.at[:, span], main.at[:, span], load_sem.at[k])
        for k, span in enumerate(spans)
    ]
    stores = [
        pltpu.make_async_copy(main.at[:, span], out_hbm.at[:, span], store_sem.at[k])
        for k, span in enumerate(spans)
    ]
    rims = pltpu.make_async_copy(arrived_hbm, arrived, rim_sem)
    rims.start()
    for copy in loads:
        copy.start()
    rims.wait()
    for k in range(steps):
        loads[k].wait()
        if k == 0:
            main[:, :rim] += arrived[0].astype(F32)
        if k == steps - 1:
            main[:, count - rim :] += arrived[1].astype(F32)
        stores[k].start()
    for copy in stores:
        copy.wait()


def on_device(
    points, charges, bases, transfers, parents, couplings, group_couplings, near_pairs, pair_count, far_list
):
    leaves = transfers.shape[1]
    count = points.shape[1]
    leaf = count // leaves
    dim, rhs, rank = points.shape[2], charges.shape[2], bases.shape[2]
    rim = REACH * leaf
    wide = count + 2 * rim
    inner, outer = lax.axis_size("inner"), lax.axis_size("outer")
    pt = jnp.swapaxes(points[0], 0, 1)
    ct = jnp.swapaxes(charges[0], 0, 1)
    pairs = jnp.swapaxes(near_pairs[0], 0, 1)
    leaf_bases = bases[0].reshape(leaves, leaf, rank)
    flat_transfers = transfers[0].reshape(leaves * rank, rank)
    dma = pltpu.SemaphoreType.DMA
    parts = leaves // 8
    halo_points, halo_charges, own, field = pl.pallas_call(
        functools.partial(exchange_kernel, inner, outer, leaves),
        out_shape=[
            jax.ShapeDtypeStruct((2, dim, rim), BF),
            jax.ShapeDtypeStruct((2, rhs, rim), BF),
            jax.ShapeDtypeStruct((rhs, count), F32),
            jax.ShapeDtypeStruct((rhs, rank), BF),
        ],
        in_specs=[HBM] * 7 + [SMEM],
        out_specs=[ANY, ANY, ANY, VMEM],
        scratch_shapes=[
            pltpu.VMEM((dim, count), BF),
            pltpu.VMEM((rhs, count), BF),
            pltpu.VMEM((leaves, leaf, rank), BF),
            pltpu.VMEM((leaves * rank, rank), BF),
            pltpu.VMEM((rank, rank), BF),
            pltpu.VMEM(couplings.shape[1:], BF),
            pltpu.VMEM(group_couplings.shape[1:], BF),
            pltpu.VMEM((rhs, count), F32),
            pltpu.VMEM((rhs, leaves * rank), BF),
            pltpu.VMEM((rhs, rank), F32),
            pltpu.VMEM((inner, rhs, rank), BF),
            pltpu.VMEM((inner, rhs, rank), F32),
            pltpu.VMEM((outer - 1, rhs, rank), F32),
            pltpu.VMEM((2, leaf, leaf), BF),
            dma((6 + parts,)),
            dma((2,)),
            dma((4,)),
            dma((4,)),
            dma((inner,)),
            dma((inner,)),
            dma((2 * (outer - 1),)),
            dma((inner,)),
            dma((inner,)),
            dma((outer - 1,)),
        ],
        compiler_params=pltpu.CompilerParams(
            vmem_limit_bytes=56 * 2**20, collective_id=0, has_side_effects=True
        ),
        name="exchange",
    )(pt, ct, leaf_bases, flat_transfers, parents[0, 0], couplings[0], group_couplings[0], far_list)
    near, halo = pl.pallas_call(
        functools.partial(pair_kernel, leaves, leaf),
        out_shape=[
            jax.ShapeDtypeStruct((rhs, count), F32),
            jax.ShapeDtypeStruct((2, rhs, rim), BF),
        ],
        in_specs=[SMEM, SMEM] + [ANY] * 4,
        out_specs=[ANY, ANY],
        scratch_shapes=[
            pltpu.VMEM((dim, wide), BF),
            pltpu.VMEM((rhs, wide), BF),
            pltpu.VMEM((EXTRA, wide), BF),
            pltpu.VMEM((EXTRA, wide), BF),
            pltpu.VMEM((rhs, wide + leaf), F32),
            pltpu.VMEM((2, leaf, leaf), BF),
            pltpu.VMEM((2, leaf, leaf), BF),
            pltpu.VMEM((2, rhs, rim), BF),
            dma((5 + parts,)),
        ],
        compiler_params=pltpu.CompilerParams(vmem_limit_bytes=56 * 2**20),
        name="pairs",
    )(pairs, pair_count, pt, ct, halo_points, halo_charges)
    main, arrived = pl.pallas_call(
        functools.partial(finish_kernel, inner),
        out_shape=[
            jax.ShapeDtypeStruct((rhs, count), F32),
            jax.ShapeDtypeStruct((2, rhs, rim), BF),
        ],
        in_specs=[ANY] * 3 + [HBM, HBM, ANY],
        out_specs=[ANY, ANY],
        scratch_shapes=[
            pltpu.VMEM((rhs, count), F32),
            pltpu.VMEM((rhs, count), F32),
            pltpu.VMEM((leaves, leaf, rank), BF),
            pltpu.VMEM((leaves * rank, rank), BF),
            pltpu.VMEM((rhs, rank), BF),
            pltpu.VMEM((rhs, leaves * rank), BF),
            dma((2 + 3 * parts,)),
            dma((parts,)),
            dma((2,)),
            dma((2,)),
        ],
        compiler_params=pltpu.CompilerParams(
            vmem_limit_bytes=56 * 2**20, collective_id=1, has_side_effects=True
        ),
        name="finish",
    )(halo, near, own, leaf_bases, flat_transfers, field)
    steps = 4
    out = pl.pallas_call(
        functools.partial(rim_kernel, steps),
        out_shape=jax.ShapeDtypeStruct((rhs, count), F32),
        in_specs=[ANY, ANY],
        out_specs=HBM,
        scratch_shapes=[
            pltpu.VMEM((rhs, count), F32),
            pltpu.VMEM((2, rhs, rim), BF),
            dma((steps,)),
            dma,
            dma((steps,)),
        ],
        compiler_params=pltpu.CompilerParams(vmem_limit_bytes=56 * 2**20),
        name="rims",
    )(main, arrived)
    return jnp.swapaxes(out, 0, 1)[None]


def solution(mesh):
    placed = (
        P("outer", "inner", None),
        P("outer", "inner", None),
        P("outer", "inner", None),
        P("outer", "inner", None, None),
        P("outer", "inner", None, None),
        P("outer", "inner", None, None),
        P("outer", None, None, None),
        P("outer", "inner", None),
        P("outer", "inner"),
        P("outer", "inner"),
    )
    return jax.shard_map(
        on_device, mesh=mesh, in_specs=placed, out_specs=P("outer", "inner", None), check_vma=False
    )
```

```python
import functools

import jax
import jax.numpy as jnp
from jax import lax
from jax.experimental import pallas as pl
from jax.experimental.pallas import tpu as pltpu
from jax.sharding import PartitionSpec as P

REACH = 4
RIDGE = 0.25
EXTRA = 16
GROUP = 4
PAIR_GROUPS = (12, 4)
BF = jnp.bfloat16
F32 = jnp.float32
VMEM = pl.BlockSpec(memory_space=pltpu.VMEM)
SMEM = pl.BlockSpec(memory_space=pltpu.SMEM)
ANY = pl.BlockSpec(memory_space=pl.ANY)
HBM = pl.BlockSpec(memory_space=pltpu.HBM)
MESH = pl.DeviceIdType.MESH


def dot(left, right, left_dim, right_dim):
    return lax.dot_general(
        left, right, (((left_dim,), (right_dim,)), ((), ())), preferred_element_type=F32
    )


def norm_rows(block):
    wide = block.astype(F32)
    total = 0.5 * jnp.sum(wide * wide, 0, keepdims=True)
    high = total.astype(BF).astype(F32)
    rest = total - high
    middle = rest.astype(BF).astype(F32)
    parts = (high, middle, rest - middle)
    row = lax.broadcasted_iota(jnp.int32, (EXTRA, block.shape[1]), 0)
    first = jnp.where((row >= 3) & (row < 6), 1.0, 0.0)
    second = jnp.where(row < 3, 1.0, 0.0)
    for k in range(3):
        first = jnp.where(row == k, -parts[k], first)
        second = jnp.where(row == 3 + k, -parts[k], second)
    return first.astype(BF), second.astype(BF)


def columns(index, width):
    return pl.ds(pl.multiple_of(index * width, width), width)


def tile_of(points, firsts, seconds, cols_a, cols_b):
    left = jnp.concatenate([points[:, cols_a], firsts[:, cols_a]], 0)
    right = jnp.concatenate([points[:, cols_b], seconds[:, cols_b]], 0)
    return jnp.exp(dot(left, right, 0, 0)).astype(BF)


def exchange_kernel(
    inner, outer, leaves,
    pt_hbm, ct_hbm, bases_hbm, transfers_hbm, parent_hbm, couplings_hbm, group_couplings_hbm, far,
    halo_points, halo_charges, near_hbm, field_out,
    points, charges, bases, transfers, parent, couplings, group_couplings, near,
    skeletons, term, slots, gathered, parts, tiles,
    load_sem, near_sem, halo_send, halo_recv, node_send, node_recv, term_send, term_recv,
    field_send, field_recv,
):
    me, group = lax.axis_index("inner"), lax.axis_index("outer")
    right, left = lax.rem(me + 1, inner), lax.rem(me + inner - 1, inner)
    rhs, count = ct_hbm.shape
    leaf = count // leaves
    rim = REACH * leaf
    rank = parent.shape[1]
    chunk = 8
    half = inner // 2
    roots = [
        (k, h, h * half + k * (half // (outer - 1))) for k in range(outer - 1) for h in range(2)
    ]
    peers = [lax.rem(me + k, inner) for k in range(1, inner)]
    sources = [lax.rem(group + k, outer) for k in range(1, outer)]
    sinks = [lax.rem(group + outer - k, outer) for k in range(1, outer)]
    loads = [
        pltpu.make_async_copy(ct_hbm, charges, load_sem.at[0]),
        pltpu.make_async_copy(transfers_hbm, transfers, load_sem.at[1]),
        pltpu.make_async_copy(pt_hbm, points, load_sem.at[2]),
        pltpu.make_async_copy(parent_hbm, parent, load_sem.at[3]),
        pltpu.make_async_copy(couplings_hbm, couplings, load_sem.at[4]),
        pltpu.make_async_copy(group_couplings_hbm, group_couplings, load_sem.at[5]),
    ]
    base_loads = [
        pltpu.make_async_copy(
            bases_hbm.at[pl.ds(k * chunk, chunk)], bases.at[pl.ds(k * chunk, chunk)], load_sem.at[6 + k]
        )
        for k in range(leaves // chunk)
    ]
    loads[0].start()
    for copy in base_loads:
        copy.start()
    loads[1].start()
    loads[3].start()
    barrier = pltpu.get_barrier_semaphore()
    for k, _, root in roots:

        @pl.when(me == root)
        def _(source=sources[k]):
            def greet(index, carry):
                pl.semaphore_signal(
                    barrier, inc=1, device_id={"inner": index, "outer": source}, device_id_type=MESH
                )
                return carry

            lax.fori_loop(0, inner, greet, 0)

    for peer in peers:
        pl.semaphore_signal(barrier, inc=1, device_id={"inner": peer}, device_id_type=MESH)

    loads[0].wait()
    for k, copy in enumerate(base_loads):
        copy.wait()
        for index in range(k * chunk, (k + 1) * chunk):
            block = charges[:, index * leaf : (index + 1) * leaf]
            skeletons[:, index * rank : (index + 1) * rank] = dot(block, bases[index], 1, 0).astype(BF)
    for k in (2, 4, 5):
        loads[k].start()
    loads[1].wait()
    node = dot(skeletons[...], transfers[...], 1, 0).astype(BF)
    slots[me] = node
    loads[3].wait()
    term[...] = dot(node, parent[...], 1, 0)
    pl.semaphore_wait(barrier, inner - 1 + len(roots))

    def remote(source, target, send, recv, **where):
        return pltpu.make_async_remote_copy(
            src_ref=source, dst_ref=target, send_sem=send, recv_sem=recv,
            device_id=where, device_id_type=MESH,
        )

    term_copies = [
        remote(term, gathered.at[me], term_send.at[at], term_recv.at[me], inner=root, outer=sinks[k])
        for at, (k, _, root) in enumerate(roots)
    ]
    for copy in term_copies:
        copy.start()
    halo_copies = [
        remote(
            source.at[:, pl.ds(begin, rim)], target, halo_send.at[k], halo_recv.at[k], inner=peer
        )
        for k, (source, target, peer, begin) in enumerate((
            (pt_hbm, halo_points.at[0], right, count - rim),
            (pt_hbm, halo_points.at[1], left, 0),
            (ct_hbm, halo_charges.at[0], right, count - rim),
            (ct_hbm, halo_charges.at[1], left, 0),
        ))
    ]
    node_copies = [
        remote(slots.at[me], slots.at[me], node_send.at[k], node_recv.at[me], inner=peer)
        for k, peer in enumerate(peers)
    ]
    field_copies = [
        [
            remote(parts.at[k], parts.at[k], field_send.at[peer], field_recv.at[k], inner=peer)
            for peer in range(h * half, (h + 1) * half)
            if peer != root
        ]
        for k, h, root in roots
    ]
    for copy in halo_copies + node_copies:
        copy.start()
    loads[2].wait()
    edge = leaf // 2

    def own_tile(index, slot):
        block = points[:, columns(index, leaf)]
        first, second = norm_rows(block)
        left_form = jnp.concatenate([block, first], 0)
        right_form = jnp.concatenate([block, second], 0)
        upper = jnp.exp(dot(left_form[:, :edge], right_form, 0, 0)).astype(BF)
        tiles[slot, :edge] = upper
        tiles[slot, edge:, :edge] = upper[:, edge:].T
        tiles[slot, edge:, edge:] = jnp.exp(
            dot(left_form[:, edge:], right_form[:, edge:], 0, 0)
        ).astype(BF)

    def diagonal(index, carry):
        for k in range(GROUP):
            at = index * GROUP + k
            own_tile(jnp.minimum(at + 1, leaves - 1), (k + 1) % 2)
            cols = columns(at, leaf)
            own = charges[:, cols]
            near[:, cols] = RIDGE * own.astype(F32) + dot(own, tiles[k % 2], 1, 0)
        return carry

    own_tile(0, 0)
    total = leaves // GROUP
    stop = 3 * total // 8
    lax.fori_loop(0, stop, diagonal, 0)
    spans = [pl.ds(0, stop * GROUP * leaf), pl.ds(stop * GROUP * leaf, (total - stop) * GROUP * leaf)]
    near_copies = [
        pltpu.make_async_copy(near.at[:, span], near_hbm.at[:, span], near_sem.at[k])
        for k, span in enumerate(spans)
    ]
    near_copies[0].start()
    loads[4].wait()
    loads[5].wait()
    for at, (k, _, root) in enumerate(roots):

        @pl.when(me == root)
        def _(at=at, k=k):
            def arrive(index, carry):
                pltpu.make_async_copy(term, gathered.at[index], term_recv.at[index]).wait()
                return carry

            lax.fori_loop(0, inner, arrive, 0)
            skeleton = jnp.sum(gathered[...], 0).astype(BF)
            parts[k] = dot(skeleton, group_couplings[sources[k]], 1, 1)
            for copy in field_copies[at]:
                copy.start()

    lax.fori_loop(stop, total, diagonal, 0)
    near_copies[1].start()
    for peer in peers:
        pltpu.make_async_copy(slots.at[me], slots.at[peer], node_recv.at[peer]).wait()
    field = jnp.zeros((rhs, rank), F32)
    for j in range(couplings.shape[0]):
        field += dot(slots[far[0, j]], couplings[j], 1, 1)
    for k in range(outer - 1):
        first_root, second_root = [root for at, _, root in roots if at == k]

        @pl.when((me != first_root) & (me != second_root))
        def _(k=k):
            pltpu.make_async_copy(parts.at[k], parts.at[k], field_recv.at[k]).wait()

    group_field = jnp.sum(parts[...], 0).astype(BF)
    field_out[...] = (field + dot(group_field, parent[...], 1, 1)).astype(BF)
    for copy in term_copies + node_copies:
        copy.wait_send()
    for at, (_, _, root) in enumerate(roots):

        @pl.when(me == root)
        def _(at=at):
            for copy in field_copies[at]:
                copy.wait_send()

    for copy in near_copies:
        copy.wait()
    for copy in halo_copies:
        copy.wait()


def pair_kernel(
    leaves, leaf,
    pairs, live, pt_hbm, ct_hbm, halo_points, halo_charges,
    out_near, out_halo,
    points, charges, firsts, seconds, totals, tiles, flipped, halo, sem,
):
    rim = REACH * leaf
    count = leaves * leaf
    chunk = 8
    spots = (pl.ds(0, rim), pl.ds(rim + count, rim))
    own = pl.ds(rim, count)
    copies = [
        pltpu.make_async_copy(halo_points.at[0], points.at[:, spots[0]], sem.at[0]),
        pltpu.make_async_copy(halo_points.at[1], points.at[:, spots[1]], sem.at[1]),
    ]
    copies += [
        pltpu.make_async_copy(
            pt_hbm.at[:, pl.ds(k * chunk * leaf, chunk * leaf)],
            points.at[:, pl.ds(rim + k * chunk * leaf, chunk * leaf)],
            sem.at[2 + k],
        )
        for k in range(leaves // chunk)
    ]
    at = len(copies)
    charge_copies = [
        pltpu.make_async_copy(ct_hbm, charges.at[:, own], sem.at[at]),
        pltpu.make_async_copy(halo_charges.at[0], charges.at[:, spots[0]], sem.at[at + 1]),
        pltpu.make_async_copy(halo_charges.at[1], charges.at[:, spots[1]], sem.at[at + 2]),
    ]
    for copy in copies + charge_copies:
        copy.start()
    totals[...] = jnp.zeros_like(totals)

    def build(index, carry):
        cols = columns(index, leaf)
        firsts[:, cols], seconds[:, cols] = norm_rows(points[:, cols])
        return carry

    spans_built = [(0, REACH), (REACH + leaves, 2 * REACH + leaves)]
    spans_built += [(REACH + k * chunk, REACH + (k + 1) * chunk) for k in range(leaves // chunk)]
    for copy, (low, high) in zip(copies, spans_built):
        copy.wait()
        lax.fori_loop(low, high, build, 0, unroll=2)
    for copy in charge_copies:
        copy.wait()
    number = live[0, 0]

    spare = leaves + 2 * REACH

    def ends(index):
        at = jnp.minimum(index, number - 1)
        return pairs[0, at] + REACH, pairs[1, at]

    def make(index, slot):
        a, b = ends(index)
        tile = tile_of(points, firsts, seconds, columns(a, leaf), columns(b, leaf))
        tiles[slot] = tile
        flipped[slot] = tile.T

    def use(index, slot):
        a, b = ends(index)
        to_a = columns(jnp.where(index < number, a, spare), leaf)
        to_b = columns(jnp.where(index < number, b, spare), leaf)
        totals[:, to_b] += dot(charges[:, columns(a, leaf)], tiles[slot], 1, 0)
        totals[:, to_a] += dot(charges[:, columns(b, leaf)], flipped[slot], 1, 0)

    make(0, 0)
    done = 0
    for size in PAIR_GROUPS:

        def block(index, carry, size=size, done=done):
            for k in range(size):
                at = done + index * size + k
                make(at + 1, (k + 1) % 2)
                use(at, k % 2)
            return carry

        left = number - done
        blocks = (left + size - 1) // size if size == PAIR_GROUPS[-1] else left // size
        lax.fori_loop(0, blocks, block, 0)
        done += blocks * size
    write = pltpu.make_async_copy(totals.at[:, own], out_near, sem.at[0])
    write.start()
    for k, spot in enumerate(spots):
        halo[k] = totals[:, spot].astype(BF)
    halo_write = pltpu.make_async_copy(halo, out_halo, sem.at[1])
    halo_write.start()
    halo_write.wait()
    write.wait()


def finish_kernel(
    inner,
    halo, near_hbm, own_hbm, bases_hbm, transfers_hbm, field_hbm,
    out, arrived,
    near, own, bases, transfers, field, leaf_fields, load_sem, store_sem, send_sem, recv_sem,
):
    me = lax.axis_index("inner")
    right, left = lax.rem(me + 1, inner), lax.rem(me + inner - 1, inner)
    leaves, leaf, rank = bases.shape
    chunk = 8
    parts = leaves // chunk
    width = chunk * leaf
    barrier = pltpu.get_barrier_semaphore()
    for peer in (left, right):
        pl.semaphore_signal(barrier, inc=1, device_id={"inner": peer}, device_id_type=MESH)
    loads = [
        pltpu.make_async_copy(transfers_hbm, transfers, load_sem.at[0]),
        pltpu.make_async_copy(field_hbm, field, load_sem.at[1 + 3 * (leaves // chunk)]),
    ]
    near_loads, own_loads, base_loads = [], [], []
    for k in range(parts):
        span = pl.ds(k * width, width)
        leaf_span = pl.ds(k * chunk, chunk)
        base_loads.append(
            pltpu.make_async_copy(bases_hbm.at[leaf_span], bases.at[leaf_span], load_sem.at[1 + k])
        )
        near_loads.append(
            pltpu.make_async_copy(near_hbm.at[:, span], near.at[:, span], load_sem.at[1 + parts + k])
        )
        own_loads.append(
            pltpu.make_async_copy(own_hbm.at[:, span], own.at[:, span], load_sem.at[1 + 2 * parts + k])
        )
    for copy in loads:
        copy.start()
    for group in zip(base_loads, near_loads, own_loads):
        for copy in group:
            copy.start()
    pl.semaphore_wait(barrier, 2)
    copies = []
    for k, peer in enumerate((left, right)):
        copy = pltpu.make_async_remote_copy(
            src_ref=halo.at[k], dst_ref=arrived.at[1 - k], send_sem=send_sem.at[k],
            recv_sem=recv_sem.at[1 - k], device_id={"inner": peer}, device_id_type=MESH,
        )
        copy.start()
        copies.append(copy)
    for copy in loads:
        copy.wait()
    leaf_fields[...] = dot(field[...], transfers[...], 1, 1).astype(BF)
    stores = []
    for k in range(parts):
        base_loads[k].wait()
        near_loads[k].wait()
        own_loads[k].wait()
        for index in range(k * chunk, (k + 1) * chunk):
            span = slice(index * leaf, (index + 1) * leaf)
            part = leaf_fields[:, index * rank : (index + 1) * rank]
            near[:, span] += own[:, span] + dot(part, bases[index], 1, 1)
        span = pl.ds(k * width, width)
        store = pltpu.make_async_copy(near.at[:, span], out.at[:, span], store_sem.at[k])
        store.start()
        stores.append(store)
    for copy in stores + copies:
        copy.wait()


def rim_kernel(steps, main_hbm, arrived_hbm, out_hbm, main, arrived, load_sem, rim_sem, store_sem):
    count = main.shape[1]
    rim = arrived.shape[2]
    width = count // steps
    spans = [pl.ds(k * width, width) for k in range(steps)]
    loads = [
        pltpu.make_async_copy(main_hbm.at[:, span], main.at[:, span], load_sem.at[k])
        for k, span in enumerate(spans)
    ]
    stores = [
        pltpu.make_async_copy(main.at[:, span], out_hbm.at[:, span], store_sem.at[k])
        for k, span in enumerate(spans)
    ]
    rims = pltpu.make_async_copy(arrived_hbm, arrived, rim_sem)
    rims.start()
    for copy in loads:
        copy.start()
    rims.wait()
    for k in range(steps):
        loads[k].wait()
        if k == 0:
            main[:, :rim] += arrived[0].astype(F32)
        if k == steps - 1:
            main[:, count - rim :] += arrived[1].astype(F32)
        stores[k].start()
    for copy in stores:
        copy.wait()


def on_device(
    points, charges, bases, transfers, parents, couplings, group_couplings, near_pairs, pair_count, far_list
):
    leaves = transfers.shape[1]
    count = points.shape[1]
    leaf = count // leaves
    dim, rhs, rank = points.shape[2], charges.shape[2], bases.shape[2]
    rim = REACH * leaf
    wide = count + 2 * rim
    inner, outer = lax.axis_size("inner"), lax.axis_size("outer")
    pt = jnp.swapaxes(points[0], 0, 1)
    ct = jnp.swapaxes(charges[0], 0, 1)
    pairs = jnp.swapaxes(near_pairs[0], 0, 1)
    leaf_bases = bases[0].reshape(leaves, leaf, rank)
    flat_transfers = transfers[0].reshape(leaves * rank, rank)
    dma = pltpu.SemaphoreType.DMA
    parts = leaves // 8
    halo_points, halo_charges, own, field = pl.pallas_call(
        functools.partial(exchange_kernel, inner, outer, leaves),
        out_shape=[
            jax.ShapeDtypeStruct((2, dim, rim), BF),
            jax.ShapeDtypeStruct((2, rhs, rim), BF),
            jax.ShapeDtypeStruct((rhs, count), F32),
            jax.ShapeDtypeStruct((rhs, rank), BF),
        ],
        in_specs=[HBM] * 7 + [SMEM],
        out_specs=[ANY, ANY, ANY, VMEM],
        scratch_shapes=[
            pltpu.VMEM((dim, count), BF),
            pltpu.VMEM((rhs, count), BF),
            pltpu.VMEM((leaves, leaf, rank), BF),
            pltpu.VMEM((leaves * rank, rank), BF),
            pltpu.VMEM((rank, rank), BF),
            pltpu.VMEM(couplings.shape[1:], BF),
            pltpu.VMEM(group_couplings.shape[1:], BF),
            pltpu.VMEM((rhs, count), F32),
            pltpu.VMEM((rhs, leaves * rank), BF),
            pltpu.VMEM((rhs, rank), F32),
            pltpu.VMEM((inner, rhs, rank), BF),
            pltpu.VMEM((inner, rhs, rank), F32),
            pltpu.VMEM((outer - 1, rhs, rank), F32),
            pltpu.VMEM((2, leaf, leaf), BF),
            dma((6 + parts,)),
            dma((2,)),
            dma((4,)),
            dma((4,)),
            dma((inner,)),
            dma((inner,)),
            dma((2 * (outer - 1),)),
            dma((inner,)),
            dma((inner,)),
            dma((outer - 1,)),
        ],
        compiler_params=pltpu.CompilerParams(
            vmem_limit_bytes=56 * 2**20, collective_id=0, has_side_effects=True
        ),
        name="exchange",
    )(pt, ct, leaf_bases, flat_transfers, parents[0, 0], couplings[0], group_couplings[0], far_list)
    near, halo = pl.pallas_call(
        functools.partial(pair_kernel, leaves, leaf),
        out_shape=[
            jax.ShapeDtypeStruct((rhs, count), F32),
            jax.ShapeDtypeStruct((2, rhs, rim), BF),
        ],
        in_specs=[SMEM, SMEM] + [ANY] * 4,
        out_specs=[ANY, ANY],
        scratch_shapes=[
            pltpu.VMEM((dim, wide), BF),
            pltpu.VMEM((rhs, wide), BF),
            pltpu.VMEM((EXTRA, wide), BF),
            pltpu.VMEM((EXTRA, wide), BF),
            pltpu.VMEM((rhs, wide + leaf), F32),
            pltpu.VMEM((2, leaf, leaf), BF),
            pltpu.VMEM((2, leaf, leaf), BF),
            pltpu.VMEM((2, rhs, rim), BF),
            dma((5 + parts,)),
        ],
        compiler_params=pltpu.CompilerParams(vmem_limit_bytes=56 * 2**20),
        name="pairs",
    )(pairs, pair_count, pt, ct, halo_points, halo_charges)
    main, arrived = pl.pallas_call(
        functools.partial(finish_kernel, inner),
        out_shape=[
            jax.ShapeDtypeStruct((rhs, count), F32),
            jax.ShapeDtypeStruct((2, rhs, rim), BF),
        ],
        in_specs=[ANY] * 3 + [HBM, HBM, ANY],
        out_specs=[ANY, ANY],
        scratch_shapes=[
            pltpu.VMEM((rhs, count), F32),
            pltpu.VMEM((rhs, count), F32),
            pltpu.VMEM((leaves, leaf, rank), BF),
            pltpu.VMEM((leaves * rank, rank), BF),
            pltpu.VMEM((rhs, rank), BF),
            pltpu.VMEM((rhs, leaves * rank), BF),
            dma((2 + 3 * parts,)),
            dma((parts,)),
            dma((2,)),
            dma((2,)),
        ],
        compiler_params=pltpu.CompilerParams(
            vmem_limit_bytes=56 * 2**20, collective_id=1, has_side_effects=True
        ),
        name="finish",
    )(halo, near, own, leaf_bases, flat_transfers, field)
    steps = 4
    out = pl.pallas_call(
        functools.partial(rim_kernel, steps),
        out_shape=jax.ShapeDtypeStruct((rhs, count), F32),
        in_specs=[ANY, ANY],
        out_specs=HBM,
        scratch_shapes=[
            pltpu.VMEM((rhs, count), F32),
            pltpu.VMEM((2, rhs, rim), BF),
            dma((steps,)),
            dma,
            dma((steps,)),
        ],
        compiler_params=pltpu.CompilerParams(vmem_limit_bytes=56 * 2**20),
        name="rims",
    )(main, arrived)
    return jnp.swapaxes(out, 0, 1)[None]


def solution(mesh):
    placed = (
        P("outer", "inner", None),
        P("outer", "inner", None),
        P("outer", "inner", None),
        P("outer", "inner", None, None),
        P("outer", "inner", None, None),
        P("outer", "inner", None, None),
        P("outer", None, None, None),
        P("outer", "inner", None),
        P("outer", "inner"),
        P("outer", "inner"),
    )
    return jax.shard_map(
        on_device, mesh=mesh, in_specs=placed, out_specs=P("outer", "inner", None), check_vma=False
    )
```
